256 devices in a mesh: row: 8 (over z_hi, x), col: 32 (over y, z_lo, core).
Axes of the slice: x: 4, y: 4, z: 8 (z_hi: 2, z_lo: 4; z = z_hi * 4 + z_lo), core: 2. Of those that a mesh axis runs over, the one named last changes fastest.
Arguments:
- image: bfloat16 [128, 2048, 96], P('row', 'col'), may hold values from -6 to 6
- kernels: float32 [2, 7, 7, 96], replicated, may hold values from -0.875 to 0.875
- gains: float32 [2, 96], replicated, may hold values from 0.5 to 1.5
- up_weights: bfloat16 [2, 96, 384], replicated, may hold values from -0.625 to 0.625
- down_weights: bfloat16 [2, 384, 96], replicated, may hold values from -0.3125 to 0.3125
- cotangent: bfloat16 [128, 2048, 96], P('row', 'col'), may hold values from -6 to 6
Outputs:
- output: bfloat16 [128, 2048, 96], P('row', 'col')
- grad_image: bfloat16 [128, 2048, 96], P('row', 'col')
- grad_kernels: float32 [2, 7, 7, 96], replicated
- grad_gains: float32 [2, 96], replicated
- grad_up: float32 [2, 96, 384], P(None, 'row', 'col')
- grad_down: float32 [2, 384, 96], P(None, 'col', 'row')
The draws below stay inside these ranges and needn't reach their ends.
All inputs are finite; a program needn't handle non-finite values.
Results may differ from the reference program's by a relative error of at most 0.029.
Values may be sent and summed in bfloat16 or wider, within the bound.
A program may use at most 64 MiB of HBM per device.

```python
import math
import jax
import jax.numpy as jnp
from jax import lax

C = 96
FF = 384
KERNEL = 7
LAYERS = 2
ROWS_DEV = 16
NH = 128
NW = 2048


def level_of(stream_key, extent, pieces, low, high):
    level = 1.0
    for position, parts in pieces:
        heights = jax.random.uniform(jax.random.fold_in(jax.random.fold_in(stream_key, 6), position), (parts,), jnp.float32, low / len(pieces), high / len(pieces))
        level = level * jnp.repeat(jnp.exp(heights), extent[position] // parts).reshape((-1,) + (1,) * (len(extent) - 1 - position))
    return level


def normal_values(key, shape, deviation, bound, pieces=(), kind=jnp.bfloat16):
    values = deviation * jax.random.normal(key, shape, jnp.float32)
    if pieces:
        values = values * level_of(key, shape, pieces, -0.22, 0.18)
    return jnp.clip(values, -bound, bound).astype(kind)


def setup_inputs(seed: int = 0) -> dict:
    splits = jax.random.split(jax.random.key(seed), 7)
    return {
        "image": normal_values(splits[0], (NH, NW, C), 1.0, 6.0, ((0, 8), (1, 32))),
        "kernels": normal_values(splits[1], (LAYERS, KERNEL, KERNEL, C), (KERNEL * KERNEL) ** -0.5, 0.875, (), jnp.float32),
        "gains": jnp.clip(jax.random.uniform(splits[2], (LAYERS, C), jnp.float32, 0.5, 1.5), 0.5, 1.5),
        "up_weights": normal_values(splits[3], (LAYERS, C, FF), C ** -0.5, 0.625),
        "down_weights": normal_values(splits[4], (LAYERS, FF, C), FF ** -0.5, 0.3125),
        "cotangent": normal_values(splits[5], (NH, NW, C), 1.0, 6.0, ((0, 8), (1, 32))),
    }


epsilon = 1e-06
inv_sqrt_two = 0.7071067811865476
inv_sqrt_two_pi = 0.3989422804014327

def depthwise(padded, kernel, tile_rows, tile_cols):
    padded_f = padded.astype(jnp.float32)
    tap_count = kernel.shape[0]
    accumulated = jnp.zeros((tile_rows, tile_cols, padded.shape[2]), jnp.float32)
    for tap_row in range(tap_count):
        for tap_col in range(tap_count):
            accumulated = accumulated + padded_f[tap_row:tap_row + tile_rows, tap_col:tap_col + tile_cols] * kernel[tap_row, tap_col]
    return accumulated

def flipped_conv(padded, kernel, tile_rows, tile_cols):
    padded_f = padded.astype(jnp.float32)
    tap_count = kernel.shape[0]
    last_tap = tap_count - 1
    accumulated = jnp.zeros((tile_rows, tile_cols, padded.shape[2]), jnp.float32)
    for tap_row in range(tap_count):
        for tap_col in range(tap_count):
            start_row = last_tap - tap_row
            start_col = last_tap - tap_col
            accumulated = accumulated + padded_f[start_row:start_row + tile_rows, start_col:start_col + tile_cols] * kernel[tap_row, tap_col]
    return accumulated

def kernel_grad(padded, conv_grad, tile_rows, tile_cols, tap_count):
    padded_f = padded.astype(jnp.float32)
    grad_f = conv_grad.astype(jnp.float32)
    rows_out = []
    for tap_row in range(tap_count):
        entries = []
        for tap_col in range(tap_count):
            entries.append(lax.optimization_barrier(jnp.sum(padded_f[tap_row:tap_row + tile_rows, tap_col:tap_col + tile_cols] * grad_f, axis=(0, 1))))
        rows_out.append(jnp.stack(entries))
    return jnp.stack(rows_out)

def normalize(conv_out):
    centred = conv_out - lax.optimization_barrier(jnp.mean(conv_out, axis=-1, keepdims=True))
    variance = lax.optimization_barrier(jnp.mean(centred * centred, axis=-1, keepdims=True))
    inverse_std = lax.rsqrt(variance + epsilon)
    return (centred * inverse_std, inverse_std)

def gelu_parts(pre):
    normal_cdf = 0.5 * (1.0 + lax.erf(pre * inv_sqrt_two))
    density = jnp.exp(-0.5 * pre * pre) * inv_sqrt_two_pi
    return (pre * normal_cdf, normal_cdf + pre * density)

def mixing(padded, kernel, gain, up_weight, tile_rows, tile_cols):
    conv_out = depthwise(padded, kernel, tile_rows, tile_cols)
    unit_vals, inverse_std = normalize(conv_out)
    normed = (unit_vals * gain).astype(jnp.bfloat16).reshape(tile_rows * tile_cols, -1)
    pre = jnp.dot(normed, up_weight, preferred_element_type=jnp.float32)
    gelu_value, gelu_slope = gelu_parts(pre)
    return (unit_vals, inverse_std, normed, gelu_value.astype(jnp.bfloat16), gelu_slope)

def forward_rows(padded, kernel, gain, up_weight, down_weight, tile_rows, tile_cols):
    unit_vals, inverse_std, normed, hidden, gelu_slope = mixing(padded, kernel, gain, up_weight, tile_rows, tile_cols)
    halo_width = kernel.shape[0] // 2
    residual = padded[halo_width:halo_width + tile_rows, halo_width:halo_width + tile_cols].astype(jnp.float32)
    branch = jnp.dot(hidden, down_weight, preferred_element_type=jnp.float32).reshape(residual.shape)
    return (residual + branch).astype(jnp.bfloat16)

def backward_rows(padded, upstream, kernel, gain, up_weight, down_weight, tile_rows, tile_cols):
    unit_vals, inverse_std, normed, hidden, gelu_slope = mixing(padded, kernel, gain, up_weight, tile_rows, tile_cols)
    channels = upstream.shape[2]
    flat_grad = upstream.reshape(tile_rows * tile_cols, channels)
    down_term = jnp.dot(hidden.T, flat_grad, preferred_element_type=jnp.float32)
    hidden_grad = jnp.dot(flat_grad, down_weight.T, preferred_element_type=jnp.float32)
    pre_grad = (hidden_grad * gelu_slope).astype(jnp.bfloat16)
    up_term = jnp.dot(normed.T, pre_grad, preferred_element_type=jnp.float32)
    normed_grad = jnp.dot(pre_grad, up_weight.T, preferred_element_type=jnp.float32).reshape(tile_rows, tile_cols, channels)
    gain_term = lax.optimization_barrier(jnp.sum(normed_grad * unit_vals, axis=(0, 1)))
    unit_grad = normed_grad * gain
    conv_grad = inverse_std * (unit_grad - lax.optimization_barrier(jnp.mean(unit_grad, axis=-1, keepdims=True)) - unit_vals * lax.optimization_barrier(jnp.mean(unit_grad * unit_vals, axis=-1, keepdims=True)))
    conv_grad = conv_grad.astype(jnp.bfloat16)
    kernel_term = kernel_grad(padded, conv_grad, tile_rows, tile_cols, kernel.shape[0])
    return (conv_grad, kernel_term, gain_term, up_term, down_term)

def reference(image, kernels, gains, up_weights, down_weights, cotangent):
    halo_width = KERNEL // 2
    block_count = NH // ROWS_DEV
    block_ids = jnp.arange(block_count, dtype=jnp.int32)
    factor = 1.0 / math.sqrt(NH * NW)
    padding = ((halo_width, halo_width), (halo_width, halo_width), (0, 0))
    current = image
    stored = []
    for layer_index in range(LAYERS):
        padded = jnp.pad(current, padding)
        stored.append(padded)

        def forward_block(block_index, padded=padded, layer_index=layer_index):
            start = (block_index * ROWS_DEV).astype(jnp.int32)
            anchor = jnp.zeros((), jnp.int32)
            slab = lax.dynamic_slice(padded, (start, anchor, anchor), (ROWS_DEV + 2 * halo_width, NW + 2 * halo_width, C))
            return forward_rows(slab, kernels[layer_index], gains[layer_index], up_weights[layer_index], down_weights[layer_index], ROWS_DEV, NW)
        current = lax.map(forward_block, block_ids).reshape(NH, NW, C)
    output = current
    gradient = cotangent
    kernel_list = [None] * LAYERS
    gain_list = [None] * LAYERS
    up_list = [None] * LAYERS
    down_list = [None] * LAYERS
    for layer_index in reversed(range(LAYERS)):
        padded = stored[layer_index]

        def backward_block(block_index, padded=padded, gradient=gradient, layer_index=layer_index):
            start = (block_index * ROWS_DEV).astype(jnp.int32)
            anchor = jnp.zeros((), jnp.int32)
            slab = lax.dynamic_slice(padded, (start, anchor, anchor), (ROWS_DEV + 2 * halo_width, NW + 2 * halo_width, C))
            upstream = lax.dynamic_slice(gradient, (start, anchor, anchor), (ROWS_DEV, NW, C))
            return backward_rows(slab, upstream, kernels[layer_index], gains[layer_index], up_weights[layer_index], down_weights[layer_index], ROWS_DEV, NW)
        conv_grads, kernel_terms, gain_terms, up_terms, down_terms = lax.map(backward_block, block_ids)
        kernel_list[layer_index] = lax.optimization_barrier(jnp.sum(kernel_terms, axis=0)) * factor
        gain_list[layer_index] = lax.optimization_barrier(jnp.sum(gain_terms, axis=0)) * factor
        up_list[layer_index] = lax.optimization_barrier(jnp.sum(up_terms, axis=0)) * factor
        down_list[layer_index] = lax.optimization_barrier(jnp.sum(down_terms, axis=0)) * factor
        padded_grad = jnp.pad(conv_grads.reshape(NH, NW, C), padding)

        def input_block(block_index, padded_grad=padded_grad, gradient=gradient, layer_index=layer_index):
            start = (block_index * ROWS_DEV).astype(jnp.int32)
            anchor = jnp.zeros((), jnp.int32)
            slab = lax.dynamic_slice(padded_grad, (start, anchor, anchor), (ROWS_DEV + 2 * halo_width, NW + 2 * halo_width, C))
            upstream = lax.dynamic_slice(gradient, (start, anchor, anchor), (ROWS_DEV, NW, C))
            return (upstream.astype(jnp.float32) + flipped_conv(slab, kernels[layer_index], ROWS_DEV, NW)).astype(jnp.bfloat16)
        gradient = lax.map(input_block, block_ids).reshape(NH, NW, C)
    return (output, gradient, jnp.stack(kernel_list), jnp.stack(gain_list), jnp.stack(up_list), jnp.stack(down_list))
```

```python
import functools
import math

import jax
import jax.numpy as jnp
from jax import lax
from jax.experimental import pallas as pl
from jax.experimental.pallas import tpu as pltpu
from jax.sharding import PartitionSpec as P

f32 = jnp.float32
bf16 = jnp.bfloat16
MESH = pl.DeviceIdType.MESH

epsilon = 1e-06
inv_sqrt_two_pi = 0.3989422804014327
tail_p = 0.275
tail_c = (
    0.11780924948816489,
    0.04211150374007564,
    0.33393224058082305,
    -0.33099335173379324,
    0.45199869046687746,
    -0.11485832782346941,
)

NX, NZH, NY, NZC = 4, 2, 4, 8
TR, TC, CH, FF, LN = 16, 64, 96, 384, 128
PX = TR * TC
ROWV = 14 * 8
PADDED = 22 * ROWV
HALO = 672
GROUP = 16


def dot(a, b, ca, cb):
    return lax.dot_general(a, b, (((ca,), (cb,)), ((), ())), preferred_element_type=f32)


def iota(shape, dim):
    return lax.broadcasted_iota(jnp.int32, shape, dim)


def kernel(
    image, kernels, gains, ups, downs, cot,
    out, gimg, gker, ggain, gup, gdown,
    img_in, cot_in, out_b, gimg_b, k_in, g_in, u_in, d_in,
    x0, x1, g0, g1, kb, gb, ub, db, stage, gradf, conv, unit, inv, normed, hidden, slope, pregrad, gradb,
    lf, rf, hsend, hrecv, wsum, sblk, rblk, sacc, s2blk, r2blk, wa, wb, wc,
    in_sem, out_sem, hs_sem, hr_sem, s1_sem, r1_sem, s2_sem, r2_sem, as_sem, ar_sem, bs_sem, br_sem, cs_sem, cr_sem,
):
    xs = (x0, x1)
    gs = (g0, g1)
    ri = lax.axis_index("row")
    ci = lax.axis_index("col")
    zh, px = ri // NX, ri % NX
    py, zc = ci // NZC, ci % NZC
    nrow, ncol = NX * NZH, NY * NZC

    def peer_a(d):
        ox = (px + d // NY) % NX
        oy = (py + d % NY) % NY
        return ox, oy, (zh * NX + ox, oy * NZC + zc)

    def peer_b(d):
        oh = (zh + d // NZC) % NZH
        oz = (zc + d % NZC) % NZC
        return oh, oz, (oh * NX + px, py * NZC + oz)

    up_r, dn_r = (ri + nrow - 1) % nrow, (ri + 1) % nrow
    lt_c, rt_c = (ci + ncol - 1) % ncol, (ci + 1) % ncol

    loads = [
        pltpu.make_async_copy(src, dst, in_sem.at[i])
        for i, (src, dst) in enumerate(
            ((image, img_in), (kernels, k_in), (gains, g_in), (ups, u_in), (downs, d_in), (cot, cot_in))
        )
    ]
    for load in loads:
        load.start()

    barrier = pltpu.get_barrier_semaphore()
    near = [(up_r, ci), (dn_r, ci), (ri, lt_c), (ri, rt_c), (up_r, lt_c), (up_r, rt_c), (dn_r, lt_c), (dn_r, rt_c)]
    everyone = near + [peer_a(d)[2] for d in range(1, GROUP)] + [peer_b(d)[2] for d in range(1, GROUP)]
    for device in everyone:
        pl.semaphore_signal(barrier, inc=1, device_id=device, device_id_type=MESH)

    stage[...] = jnp.zeros_like(stage)
    gb[...] = jnp.zeros_like(gb)
    ub[...] = jnp.zeros_like(ub)
    db[...] = jnp.zeros_like(db)
    kb[...] = jnp.zeros_like(kb)

    loads[0].wait()
    stage[:, 0:CH] = img_in[...].astype(f32)

    def spread(r, _):
        for j in range(8):
            x0[pl.ds(pl.multiple_of((r + 3) * ROWV + (3 + j) * 8, 8), 8), :] = stage[
                pl.ds(r * TC + j, 8, stride=8), :
            ]
        return 0

    lax.fori_loop(0, TR, spread, 0)

    pl.semaphore_wait(barrier, len(everyone))

    def send_halo(e, x):
        for q in range(3):
            hsend[e, q * 64 : q * 64 + 64] = x[(3 + q) * ROWV + 24 : (3 + q) * ROWV + 88, :].astype(bf16)
            hsend[e, 192 + q * 64 : 256 + q * 64] = x[(16 + q) * ROWV + 24 : (16 + q) * ROWV + 88, :].astype(bf16)
            hsend[e, 384 + q * 16 : 400 + q * 16] = x[
                pl.ds(3 * ROWV + (3 + q) * 8, TR, stride=ROWV), :
            ].astype(bf16)
            hsend[e, 432 + q * 16 : 448 + q * 16] = x[
                pl.ds(3 * ROWV + (8 + q) * 8 + 7, TR, stride=ROWV), :
            ].astype(bf16)
        for source, size, target, device in (
            (0, 192, 192, (up_r, ci)),
            (192, 192, 0, (dn_r, ci)),
            (384, 48, 432, (ri, lt_c)),
            (432, 48, 384, (ri, rt_c)),
            (384, 48, 624, (up_r, lt_c)),
            (432, 48, 576, (up_r, rt_c)),
            (384, 48, 528, (dn_r, lt_c)),
            (432, 48, 480, (dn_r, rt_c)),
        ):
            pltpu.make_async_remote_copy(
                src_ref=hsend.at[e, pl.ds(source, size)],
                dst_ref=hrecv.at[e, pl.ds(target, size)],
                send_sem=hs_sem.at[e],
                recv_sem=hr_sem.at[e],
                device_id=device,
                device_id_type=MESH,
            ).start()

    m_up = jnp.where(ri == 0, 0.0, 1.0).astype(f32)
    m_dn = jnp.where(ri == nrow - 1, 0.0, 1.0).astype(f32)
    m_lt = jnp.where(ci == 0, 0.0, 1.0).astype(f32)
    m_rt = jnp.where(ci == ncol - 1, 0.0, 1.0).astype(f32)
    first = iota((8, LN), 0) == 0
    last = iota((8, LN), 0) == 7

    def fill_halo(e, x):
        pltpu.make_async_copy(hrecv.at[e], hrecv.at[e], hr_sem.at[e]).wait()
        for q in range(3):
            x[q * ROWV + 24 : q * ROWV + 88, :] = hrecv[e, q * 64 : q * 64 + 64].astype(f32) * m_up
            x[(19 + q) * ROWV + 24 : (19 + q) * ROWV + 88, :] = (
                hrecv[e, 192 + q * 64 : 256 + q * 64].astype(f32) * m_dn
            )
            o = q * 24
            for ref, m, mid, upper, lower in ((lf, m_lt, 384, 480, 576), (rf, m_rt, 432, 528, 624)):
                ref[o + 3 : o + 19, :] = hrecv[e, mid + q * 16 : mid + q * 16 + 16].astype(f32) * m
                ref[o : o + 3, :] = hrecv[e, upper + q * 16 : upper + q * 16 + 16].astype(f32)[13:16] * (m * m_up)
                ref[o + 19 : o + 22, :] = hrecv[e, lower + q * 16 : lower + q * 16 + 16].astype(f32)[0:3] * (m * m_dn)

        def row(r, _):
            base = r * ROWV
            for q in range(3):
                v = x[pl.ds(pl.multiple_of(base + (8 + q) * 8, 8), 8), :]
                edge = jnp.broadcast_to(lf[pl.ds(q * 24 + r, 1), :], (8, LN))
                x[pl.ds(pl.multiple_of(base + q * 8, 8), 8), :] = jnp.where(first, edge, pltpu.roll(v, 1, 0))
                v = x[pl.ds(pl.multiple_of(base + (3 + q) * 8, 8), 8), :]
                edge = jnp.broadcast_to(rf[pl.ds(q * 24 + r, 1), :], (8, LN))
                x[pl.ds(pl.multiple_of(base + (11 + q) * 8, 8), 8), :] = jnp.where(last, edge, pltpu.roll(v, 7, 0))
            return 0

        lax.fori_loop(0, 22, row, 0, unroll=2)

    def conv_row(x, layer, r, flip):
        acc = None
        for a in range(7):
            xa = x[pl.ds(pl.multiple_of((r + a) * ROWV, 8), ROWV), :].reshape(14, 8, LN)
            for b in range(7):
                t = a * 8 + b
                tap = (6 - a) * 8 + 6 - b if flip else t
                term = xa[b : b + 8] * kb[layer, tap][None]
                acc = term if acc is None else acc + term
        return acc

    send_halo(0, x0)

    for load in loads[1:]:
        load.wait()
    for layer in range(2):
        gb[layer, 0:1, 0:CH] = g_in[layer : layer + 1, :]
        ub[layer, 0:CH, :] = u_in[layer]
        db[layer, :, 0:CH] = d_in[layer]
        for a in range(7):
            for b in range(7):
                kb[layer, a * 8 + b, :, 0:CH] = jnp.broadcast_to(k_in[layer, a, b : b + 1, :], (8, CH))
    stage[:, 0:CH] = cot_in[...].astype(f32)

    def spread_cot(r, _):
        for j in range(8):
            gradf[pl.ds(pl.multiple_of(r * TC + j * 8, 8), 8), :] = stage[pl.ds(r * TC + j, 8, stride=8), :]
        return 0

    lax.fori_loop(0, TR, spread_cot, 0)
    lane_ok = jnp.where(iota((8, LN), 1) < CH, 1.0, 0.0).astype(f32)[0:1]

    CHUNK = 256
    ROWS = CHUNK // TC

    def forward(layer):
        x = xs[layer]

        def conv_step(r, _):
            conv[pl.ds(pl.multiple_of(r * TC, TC), TC), :] = conv_row(x, layer, r, False).reshape(TC, LN)
            return 0

        lax.fori_loop(0, TR, conv_step, 0)

        def mix(c, _):
            here = pl.ds(pl.multiple_of(c * CHUNK, CHUNK), CHUNK)
            v = conv[here, :]
            mean = jnp.sum(v, axis=1, keepdims=True) * (1.0 / CH)
            centred = (v - mean) * lane_ok
            variance = jnp.sum(centred * centred, axis=1, keepdims=True) * (1.0 / CH)
            inverse = lax.rsqrt(variance + epsilon)
            u = centred * inverse
            unit[layer, here, :] = u
            inv[layer, here, :] = jnp.broadcast_to(inverse, (CHUNK, LN))
            n = (u * gb[layer, 0:1, :]).astype(bf16)
            normed[layer, here, :] = n
            pre = dot(n, ub[layer], 1, 0)
            z = jnp.abs(pre)
            e = jnp.exp(-0.5 * pre * pre)
            t = 1.0 / (1.0 + tail_p * z)
            poly = tail_c[5] * t + tail_c[4]
            for k in (3, 2, 1, 0):
                poly = poly * t + tail_c[k]
            tail = poly * t * e
            cdf = jnp.where(pre >= 0.0, 1.0 - tail, tail)
            h = (pre * cdf).astype(bf16)
            hidden[layer, here, :] = h
            slope[layer, here, :] = cdf + pre * (e * inv_sqrt_two_pi)
            branch = dot(h, db[layer], 1, 0)
            for r in range(ROWS):
                start = (c * ROWS + r + 3) * ROWV + 24
                centre = x[pl.ds(pl.multiple_of(start, 8), TC), :]
                value = (centre + branch[r * TC : r * TC + TC]).astype(bf16).astype(f32)
                if layer == 0:
                    x1[pl.ds(pl.multiple_of(start, 8), TC), :] = value
                else:
                    for j in range(8):
                        stage[pl.ds((c * ROWS + r) * TC + j, 8, stride=8), :] = value[j * 8 : j * 8 + 8]
            return 0

        lax.fori_loop(0, PX // CHUNK, mix, 0)

    fill_halo(0, x0)
    forward(0)
    send_halo(1, x1)
    fill_halo(1, x1)
    forward(1)
    out_b[...] = stage[:, 0:CH].astype(bf16)
    out_copy = pltpu.make_async_copy(out_b, out, out_sem.at[0])
    out_copy.start()

    def backward(layer):
        x, g = xs[layer], gs[layer]

        def mix(c, total):
            here = pl.ds(pl.multiple_of(c * CHUNK, CHUNK), CHUNK)
            gr = gradf[here, :].astype(bf16)
            gradb[here, :] = gr
            pg = (dot(gr, db[layer], 1, 1) * slope[layer, here, :]).astype(bf16)
            pregrad[here, :] = pg
            ng = dot(pg, ub[layer], 1, 1)
            u = unit[layer, here, :]
            gain_rows = jnp.sum((ng * u).reshape(CHUNK // 8, 8, LN), axis=0)
            m = ng * gb[layer, 0:1, :]
            mean_m = jnp.sum(m, axis=1, keepdims=True) * (1.0 / CH)
            mean_mu = jnp.sum(m * u, axis=1, keepdims=True) * (1.0 / CH)
            cg = inv[layer, here, :] * (m - mean_m - u * mean_mu)
            cg = cg.astype(bf16).astype(f32)
            for r in range(ROWS):
                start = (c * ROWS + r + 3) * ROWV + 24
                g[pl.ds(pl.multiple_of(start, 8), TC), :] = cg[r * TC : r * TC + TC]
            return total + gain_rows

        gain = lax.fori_loop(0, PX // CHUNK, mix, jnp.zeros((8, LN), f32))
        send_halo(3 - layer, g)

        up_sum = dot(normed[layer], pregrad[...], 0, 0)
        down_sum = dot(gradb[...], hidden[layer], 0, 0)
        both = jnp.concatenate([up_sum, down_sum], axis=0).astype(bf16)
        o, k = iota((192, 256), 0), iota((192, 256), 1)
        q = (o * 43691) >> 19
        i = o - q * 12
        pick = (k == ((q >> 1) & 1) * 128 + (q & 1) * 48 + (q >> 2) * 12 + i).astype(f32).astype(bf16)
        rows = dot(pick, both, 1, 0).astype(bf16)
        for y in range(NY):
            k, n = iota((FF, LN), 0), iota((FF, LN), 1)
            pick = ((k == n + y * 96) & (n < 96)).astype(f32).astype(bf16)
            sblk[layer, y] = dot(rows, pick, 1, 0).astype(bf16)
        for d in range(1, GROUP):
            ox, oy, device = peer_a(d)
            pltpu.make_async_remote_copy(
                src_ref=sblk.at[layer, oy, pl.ds(pl.multiple_of(ox * 48, 16), 48)],
                dst_ref=rblk.at[layer, d - 1],
                send_sem=s1_sem.at[layer],
                recv_sem=r1_sem.at[layer],
                device_id=device,
                device_id_type=MESH,
            ).start()

        def tap_row(a, _):
            def add(r, acc):
                xa = x[pl.ds(pl.multiple_of((r + a) * ROWV, 8), ROWV), :].reshape(14, 8, LN)
                gr = g[pl.ds(pl.multiple_of((r + 3) * ROWV + 24, 8), TC), :].reshape(8, 8, LN)
                return tuple(acc[b] + jnp.sum(xa[b : b + 8] * gr, axis=0) for b in range(7))

            acc = lax.fori_loop(0, TR, add, tuple(jnp.zeros((8, LN), f32) for _ in range(7)))
            wsum[pl.ds(pl.multiple_of(a * 64, 64), 56), :] = jnp.concatenate(acc, axis=0)
            return 0

        lax.fori_loop(0, 7, tap_row, 0)
        wsum[56:64, :] = gain
        for a in range(7):
            rows8 = jnp.sum(wsum[a * 64 : a * 64 + 64, :].reshape(8, 8, LN), axis=1)
            wa[layer * 64 + a * 8 : layer * 64 + a * 8 + 8, :] = rows8

    def input_grad(layer):
        g = gs[layer]

        def step(r, _):
            here = pl.ds(pl.multiple_of(r * TC, TC), TC)
            value = gradf[here, :] + conv_row(g, layer, r, True).reshape(TC, LN)
            value = value.astype(bf16).astype(f32)
            if layer == 1:
                gradf[here, :] = value
            else:
                for j in range(8):
                    stage[pl.ds(r * TC + j, 8, stride=8), :] = value[j * 8 : j * 8 + 8]
            return 0

        lax.fori_loop(0, TR, step, 0)

    sacc[...] = jnp.zeros_like(sacc)
    wa[...] = jnp.zeros_like(wa)
    wsum[...] = jnp.zeros_like(wsum)

    def gather_blocks(layer):
        pltpu.make_async_copy(rblk.at[layer], rblk.at[layer], r1_sem.at[layer]).wait()
        total = sblk[layer, py, pl.ds(pl.multiple_of(px * 48, 16), 48)].astype(f32)
        for d in range(1, GROUP):
            total = total + rblk[layer, d - 1].astype(f32)
        sacc[layer * 48 : layer * 48 + 48, :] = total

    backward(1)
    fill_halo(2, g1)
    input_grad(1)
    gather_blocks(1)
    backward(0)

    part = pl.ds(0, (GROUP - 1) * 8)
    mine_a = px * NY + py
    mine_b = zh * NZC + zc
    for d in range(1, GROUP):
        ox, oy, device = peer_a(d)
        pltpu.make_async_remote_copy(
            src_ref=wa.at[pl.ds(pl.multiple_of((ox * NY + oy) * 8, 8), 8)],
            dst_ref=wb.at[0, pl.ds((d - 1) * 8, 8)],
            send_sem=as_sem,
            recv_sem=ar_sem,
            device_id=device,
            device_id_type=MESH,
        ).start()

    fill_halo(3, g0)
    gather_blocks(0)
    o, k = iota((LN, LN), 0), iota((LN, LN), 1)
    pick = ((k == (o >> 4) * 12 + (o & 15)) & ((o & 15) < 12)).astype(f32).astype(bf16)
    s2blk[...] = dot(pick, sacc[...].astype(bf16), 1, 1).astype(bf16)
    for d in range(1, GROUP):
        oh, oz, device = peer_b(d)
        pltpu.make_async_remote_copy(
            src_ref=s2blk.at[pl.ds(pl.multiple_of(oz * 16, 16), 16)],
            dst_ref=r2blk.at[pl.ds((d - 1) * 16, 16)],
            send_sem=s2_sem,
            recv_sem=r2_sem,
            device_id=device,
            device_id_type=MESH,
        ).start()

    pltpu.make_async_copy(wb.at[0, part], wb.at[0, part], ar_sem).wait()
    total = wa[pl.ds(pl.multiple_of(mine_a * 8, 8), 8), :]
    for d in range(1, GROUP):
        total = total + wb[0, (d - 1) * 8 : d * 8, :]
    wb[1, pl.ds(pl.multiple_of(mine_b * 8, 8), 8), :] = total
    for d in range(1, GROUP):
        pltpu.make_async_remote_copy(
            src_ref=wb.at[1, pl.ds(pl.multiple_of(mine_b * 8, 8), 8)],
            dst_ref=wb.at[1, pl.ds(pl.multiple_of(mine_b * 8, 8), 8)],
            send_sem=bs_sem,
            recv_sem=br_sem,
            device_id=peer_b(d)[2],
            device_id_type=MESH,
        ).start()

    input_grad(0)
    gimg_b[...] = stage[:, 0:CH].astype(bf16)
    gimg_copy = pltpu.make_async_copy(gimg_b, gimg, out_sem.at[1])
    gimg_copy.start()

    pltpu.make_async_copy(wb.at[1, part], wb.at[1, part], br_sem).wait()
    total = wb[1, 0:8, :]
    for d in range(1, GROUP):
        total = total + wb[1, d * 8 : d * 8 + 8, :]
    wc[pl.ds(pl.multiple_of(mine_a * 8, 8), 8), :] = total * (1.0 / 512.0)
    for d in range(1, GROUP):
        pltpu.make_async_remote_copy(
            src_ref=wc.at[pl.ds(pl.multiple_of(mine_a * 8, 8), 8)],
            dst_ref=wc.at[pl.ds(pl.multiple_of(mine_a * 8, 8), 8)],
            send_sem=cs_sem,
            recv_sem=cr_sem,
            device_id=peer_a(d)[2],
            device_id_type=MESH,
        ).start()

    pltpu.make_async_copy(r2blk, r2blk, r2_sem).wait()
    total = s2blk[pl.ds(pl.multiple_of(zc * 16, 16), 16), :].astype(f32)
    for d in range(1, GROUP):
        total = total + r2blk[(d - 1) * 16 : d * 16, :].astype(f32)
    total = total * (1.0 / 512.0)
    turned = jnp.concatenate([total, jnp.zeros((LN - 16, LN), f32)], axis=0).T
    for layer in range(2):
        o = layer * 48
        gup[layer] = jnp.where(zh == 0, turned[o : o + 12, 0:12], turned[o + 12 : o + 24, 0:12])
        gdown[layer] = jnp.where(zh == 0, total[0:12, o + 24 : o + 36], total[0:12, o + 36 : o + 48])

    pltpu.make_async_copy(wc.at[part], wc.at[part], cr_sem).wait()
    for layer in range(2):
        for a in range(7):
            gker[layer, a] = wc[layer * 64 + a * 8 : layer * 64 + a * 8 + 7, 0:CH]
        ggain[layer : layer + 1, :] = wc[layer * 64 + 7 : layer * 64 + 8, 0:CH]

    for e in range(4):
        pltpu.make_async_copy(hsend.at[e], hsend.at[e], hs_sem.at[e]).wait()
    for layer in range(2):
        pltpu.make_async_copy(rblk.at[layer], rblk.at[layer], s1_sem.at[layer]).wait()
    pltpu.make_async_copy(r2blk, r2blk, s2_sem).wait()
    pltpu.make_async_copy(wb.at[0, part], wb.at[0, part], as_sem).wait()
    pltpu.make_async_copy(wb.at[1, part], wb.at[1, part], bs_sem).wait()
    pltpu.make_async_copy(wc.at[part], wc.at[part], cs_sem).wait()
    out_copy.wait()
    gimg_copy.wait()


def per_device(image, kernels, gains, ups, downs, cot):
    vmem = pltpu.VMEM
    dma = pltpu.SemaphoreType.DMA
    any_spec = pl.BlockSpec(memory_space=pl.ANY)
    vmem_spec = pl.BlockSpec(memory_space=pltpu.VMEM)
    outs = pl.pallas_call(
        kernel,
        out_shape=(
            jax.ShapeDtypeStruct((PX, CH), bf16),
            jax.ShapeDtypeStruct((PX, CH), bf16),
            jax.ShapeDtypeStruct((2, 7, 7, CH), f32),
            jax.ShapeDtypeStruct((2, CH), f32),
            jax.ShapeDtypeStruct((2, 12, 12), f32),
            jax.ShapeDtypeStruct((2, 12, 12), f32),
        ),
        in_specs=[any_spec] * 6,
        out_specs=(any_spec, any_spec, vmem_spec, vmem_spec, vmem_spec, vmem_spec),
        scratch_shapes=[
            vmem((PX, CH), bf16),
            vmem((PX, CH), bf16),
            vmem((PX, CH), bf16),
            vmem((PX, CH), bf16),
            vmem((2, 7, 7, CH), f32),
            vmem((2, CH), f32),
            vmem((2, CH, FF), bf16),
            vmem((2, FF, CH), bf16),
            vmem((PADDED, LN), f32),
            vmem((PADDED, LN), f32),
            vmem((PADDED, LN), f32),
            vmem((PADDED, LN), f32),
            vmem((2, 56, 8, LN), f32),
            vmem((2, 8, LN), f32),
            vmem((2, LN, FF), bf16),
            vmem((2, FF, LN), bf16),
            vmem((PX, LN), f32),
            vmem((PX, LN), f32),
            vmem((PX, LN), f32),
            vmem((2, PX, LN), f32),
            vmem((2, PX, LN), f32),
            vmem((2, PX, LN), bf16),
            vmem((2, PX, FF), bf16),
            vmem((2, PX, FF), f32),
            vmem((PX, FF), bf16),
            vmem((PX, LN), bf16),
            vmem((72, LN), f32),
            vmem((72, LN), f32),
            vmem((4, HALO, LN), bf16),
            vmem((4, HALO, LN), bf16),
            vmem((7 * 64, LN), f32),
            vmem((2, NY, 192, LN), bf16),
            vmem((2, GROUP - 1, 48, LN), bf16),
            vmem((LN, LN), f32),
            vmem((LN, LN), bf16),
            vmem(((GROUP - 1) * 16, LN), bf16),
            vmem((LN, LN), f32),
            vmem((2, LN, LN), f32),
            vmem((LN, LN), f32),
            dma((6,)),
            dma((2,)),
            dma((4,)),
            dma((4,)),
            dma((2,)),
            dma((2,)),
            dma,
            dma,
            dma,
            dma,
            dma,
            dma,
            dma,
            dma,
        ],
        compiler_params=pltpu.CompilerParams(
            collective_id=0, has_side_effects=True, vmem_limit_bytes=48 * 1024 * 1024
        ),
        cost_estimate=pl.CostEstimate(flops=2000000000, bytes_accessed=2000000, transcendentals=1600000),
    )(image.reshape(PX, CH), kernels, gains, ups, downs, cot.reshape(PX, CH))
    return (outs[0].reshape(TR, TC, CH), outs[1].reshape(TR, TC, CH)) + tuple(outs[2:])


def solution(mesh):
    placed = (P("row", "col", None), P(), P(), P(), P(), P("row", "col", None))
    return jax.shard_map(
        per_device,
        mesh=mesh,
        in_specs=placed,
        out_specs=(
            P("row", "col", None),
            P("row", "col", None),
            P(),
            P(),
            P(None, "row", "col"),
            P(None, "col", "row"),
        ),
        check_vma=False,
    )
```

```python
import functools
import math

import jax
import jax.numpy as jnp
from jax import lax
from jax.experimental import pallas as pl
from jax.experimental.pallas import tpu as pltpu
from jax.sharding import PartitionSpec as P

f32 = jnp.float32
bf16 = jnp.bfloat16
MESH = pl.DeviceIdType.MESH

epsilon = 1e-06
inv_sqrt_two_pi = 0.3989422804014327
half_log2e = -0.7213475204444817
tail_p = 0.275
tail_c = (
    0.11780924948816489,
    0.04211150374007564,
    0.33393224058082305,
    -0.33099335173379324,
    0.45199869046687746,
    -0.11485832782346941,
)

NX, NZH, NY, NZC = 4, 2, 4, 8
TR, TC, CH, FF, LN = 16, 64, 96, 384, 128
PX = TR * TC
ROWV = 14 * 8
PADDED = 22 * ROWV
HALO = 544
GROUP = 16


def reciprocal(d):
    return pltpu.reciprocal(d, approx=True)


def dot(a, b, ca, cb):
    return lax.dot_general(a, b, (((ca,), (cb,)), ((), ())), preferred_element_type=f32)


def iota(shape, dim):
    return lax.broadcasted_iota(jnp.int32, shape, dim)


def kernel(
    image, kernels, gains, ups, downs, cot,
    out, gimg, gker, ggain, gup, gdown,
    img_in, cot_in, out_b, gimg_b, k_in, g_in, u_in, d_in,
    x0, x1, g0, g1, kb, gb, ub, db, stage, gradf, conv, unit, inv, normed, hidden, slope, pregrad, gradb,
    lf, rf, corner, hsend, hrecv, gain, wsum, sblk, rblk, sacc, s2blk, r2blk, wa, wpair, wgroup, wline, wall,
    in_sem, out_sem, hs_sem, hc_sem, hr_sem, s1_sem, r1_sem, s2_sem, r2_sem, ps_sem, pr_sem, as_sem, ar_sem,
    zs_sem, zr_sem, cs_sem, cr_sem,
):
    xs = (x0, x1)
    gs = (g0, g1)
    ri = lax.axis_index("row")
    ci = lax.axis_index("col")
    zh, px = ri // NX, ri % NX
    py, zc = ci // NZC, ci % NZC
    core = ci % 2
    nrow, ncol = NX * NZH, NY * NZC

    def peer_a(d):
        ox = (px + d // NY) % NX
        oy = (py + d % NY) % NY
        return ox, oy, (zh * NX + ox, oy * NZC + zc)

    def peer_b(d):
        oh = (zh + d // NZC) % NZH
        oz = (zc + d % NZC) % NZC
        return oz, (oh * NX + px, py * NZC + oz)

    def send(src, dst, send_sem, recv_sem, device):
        pltpu.make_async_remote_copy(
            src_ref=src, dst_ref=dst, send_sem=send_sem, recv_sem=recv_sem, device_id=device, device_id_type=MESH
        ).start()

    def await_bytes(ref, sem):
        pltpu.make_async_copy(ref, ref, sem).wait()

    up_r, dn_r = (ri + nrow - 1) % nrow, (ri + 1) % nrow
    lt_c, rt_c = (ci + ncol - 1) % ncol, (ci + 1) % ncol
    pair = (ri, ci + 1 - 2 * core)

    loads = [
        pltpu.make_async_copy(src, dst, in_sem.at[i])
        for i, (src, dst) in enumerate(
            ((image, img_in), (kernels, k_in), (gains, g_in), (ups, u_in), (downs, d_in), (cot, cot_in))
        )
    ]
    for load in loads:
        load.start()

    barrier = pltpu.get_barrier_semaphore()
    near = [(up_r, ci), (dn_r, ci), (ri, lt_c), (ri, rt_c), (up_r, lt_c), (up_r, rt_c), (dn_r, lt_c), (dn_r, rt_c)]
    everyone = near + [peer_a(d)[2] for d in range(1, GROUP)] + [peer_b(d)[1] for d in range(1, GROUP)]
    for device in everyone:
        pl.semaphore_signal(barrier, inc=1, device_id=device, device_id_type=MESH)

    def rows(start, size):
        return pl.ds(pl.multiple_of(start, 8), size)

    def pack_halo(e, x):
        for q in range(3):
            left, right = (3 + q) * 8, (8 + q) * 8 + 7
            hsend[e, q * 16 : q * 16 + 16] = x[pl.ds(3 * ROWV + left, TR, stride=ROWV), :].astype(bf16)
            hsend[e, 48 + q * 16 : 64 + q * 16] = x[pl.ds(3 * ROWV + right, TR, stride=ROWV), :].astype(bf16)
            top, bottom = (3 + q) * ROWV + 24, (16 + q) * ROWV + 24
            hsend[e, 96 + q * 64 : 160 + q * 64] = x[top : top + 64, :].astype(bf16)
            hsend[e, 288 + q * 64 : 352 + q * 64] = x[bottom : bottom + 64, :].astype(bf16)
            for c, start in enumerate(
                (3 * ROWV + left, 3 * ROWV + right, 16 * ROWV + left, 16 * ROWV + right)
            ):
                corner[c * 16 + q * 4 : c * 16 + q * 4 + 3, :] = x[pl.ds(start, 3, stride=ROWV), :]
        hsend[e, 480:544] = corner[...].astype(bf16)

    def start_halo(e):
        for source, size, target, sem, device in (
            (0, 48, 48, hc_sem, (ri, lt_c)),
            (48, 48, 0, hc_sem, (ri, rt_c)),
            (96, 192, 288, hr_sem, (up_r, ci)),
            (288, 192, 96, hr_sem, (dn_r, ci)),
            (480, 16, 528, hr_sem, (up_r, lt_c)),
            (496, 16, 512, hr_sem, (up_r, rt_c)),
            (512, 16, 496, hr_sem, (dn_r, lt_c)),
            (528, 16, 480, hr_sem, (dn_r, rt_c)),
        ):
            send(hsend.at[e, pl.ds(source, size)], hrecv.at[e, pl.ds(target, size)], hs_sem.at[e], sem.at[e], device)

    m_up = jnp.where(ri == 0, 0.0, 1.0).astype(f32)
    m_dn = jnp.where(ri == nrow - 1, 0.0, 1.0).astype(f32)
    m_lt = jnp.where(ci == 0, 0.0, 1.0).astype(f32)
    m_rt = jnp.where(ci == ncol - 1, 0.0, 1.0).astype(f32)
    first = iota((8, LN), 0) == 0
    last = iota((8, LN), 0) == 7

    def extend_row(x, r):
        base = r * ROWV
        for q in range(3):
            v = x[rows(base + (8 + q) * 8, 8), :]
            edge = jnp.broadcast_to(lf[pl.ds(q * 24 + r, 1), :], (8, LN))
            x[rows(base + q * 8, 8), :] = jnp.where(first, edge, pltpu.roll(v, 1, 0))
            v = x[rows(base + (3 + q) * 8, 8), :]
            edge = jnp.broadcast_to(rf[pl.ds(q * 24 + r, 1), :], (8, LN))
            x[rows(base + (11 + q) * 8, 8), :] = jnp.where(last, edge, pltpu.roll(v, 7, 0))

    def fill_cols(e, x):
        await_bytes(hrecv.at[e, pl.ds(0, 96)], hc_sem.at[e])
        for q in range(3):
            lf[q * 24 + 3 : q * 24 + 19, :] = hrecv[e, q * 16 : q * 16 + 16].astype(f32) * m_lt
            rf[q * 24 + 3 : q * 24 + 19, :] = hrecv[e, 48 + q * 16 : 64 + q * 16].astype(f32) * m_rt

        def step(i, _):
            extend_row(x, 3 + 2 * i)
            extend_row(x, 4 + 2 * i)
            return 0

        lax.fori_loop(0, TR // 2, step, 0)

    def fill_rows(e, x):
        await_bytes(hrecv.at[e, pl.ds(96, 448)], hr_sem.at[e])
        corners = hrecv[e, 480:544].astype(f32)
        for q in range(3):
            x[q * ROWV + 24 : q * ROWV + 88, :] = hrecv[e, 96 + q * 64 : 160 + q * 64].astype(f32) * m_up
            x[(19 + q) * ROWV + 24 : (19 + q) * ROWV + 88, :] = (
                hrecv[e, 288 + q * 64 : 352 + q * 64].astype(f32) * m_dn
            )
            o = q * 24
            for c, (ref, m, at) in enumerate(
                ((lf, m_lt * m_up, o), (rf, m_rt * m_up, o), (lf, m_lt * m_dn, o + 19), (rf, m_rt * m_dn, o + 19))
            ):
                ref[at : at + 3, :] = corners[c * 16 + q * 4 : c * 16 + q * 4 + 3] * m

        def step(i, _):
            extend_row(x, i)
            extend_row(x, i + 19)
            return 0

        lax.fori_loop(0, 3, step, 0)

    def conv_rows(x, layer, r, count, flip):
        accs = [None] * count
        for a in range(6 + count):
            xa = x[rows((r + a) * ROWV, ROWV), :].reshape(14, 8, LN)
            for b in range(7):
                for n in range(count):
                    if 0 <= a - n < 7:
                        tap = (6 - a + n) * 8 + 6 - b if flip else (a - n) * 8 + b
                        term = xa[b : b + 8] * kb[layer, tap][None]
                        accs[n] = term if accs[n] is None else accs[n] + term
        return accs

    stage[...] = jnp.zeros_like(stage)
    corner[...] = jnp.zeros_like(corner)
    gb[...] = jnp.zeros_like(gb)
    ub[...] = jnp.zeros_like(ub)
    db[...] = jnp.zeros_like(db)
    kb[...] = jnp.zeros_like(kb)
    gain[...] = jnp.zeros_like(gain)
    sacc[...] = jnp.zeros_like(sacc)
    wsum[...] = jnp.zeros_like(wsum)
    wa[...] = jnp.zeros_like(wa)

    loads[0].wait()
    stage[:, 0:CH] = img_in[...].astype(f32)

    def spread(r, _):
        for j in range(8):
            x0[rows((r + 3) * ROWV + (3 + j) * 8, 8), :] = stage[pl.ds(r * TC + j, 8, stride=8), :]
        return 0

    lax.fori_loop(0, TR, spread, 0)
    pack_halo(0, x0)
    for load in loads[1:]:
        load.wait()
    for layer in range(2):
        gb[layer, 0:1, 0:CH] = g_in[layer : layer + 1, :]
        ub[layer, 0:CH, :] = u_in[layer]
        db[layer, 0:CH, :] = d_in[layer]
        for a in range(7):
            for b in range(7):
                kb[layer, a * 8 + b, :, 0:CH] = jnp.broadcast_to(k_in[a, b, layer : layer + 1, :], (8, CH))
    stage[:, 0:CH] = cot_in[...].astype(f32)

    def spread_cot(r, _):
        for j in range(8):
            gradf[rows(r * TC + j * 8, 8), :] = stage[pl.ds(r * TC + j, 8, stride=8), :]
        return 0

    lax.fori_loop(0, TR, spread_cot, 0)
    lane_ok = jnp.where(iota((8, LN), 1) < CH, 1.0, 0.0).astype(f32)[0:1]

    pl.semaphore_wait(barrier, len(everyone))
    start_halo(0)

    def each(inner, conv_step, mix_step):
        if inner:
            if conv_step is not None:
                lax.fori_loop(0, 5, lambda i, c: (conv_step(3 + 2 * i, 2), c)[1], 0)
            if mix_step is not None:
                lax.fori_loop(0, 2, lambda i, c: (mix_step(3 + 5 * i, 5), c)[1], 0)
        else:
            if conv_step is not None:
                lax.fori_loop(0, 2, lambda i, c: (conv_step(13 * i, 3), c)[1], 0)
            if mix_step is not None:
                lax.fori_loop(0, 2, lambda i, c: (mix_step(13 * i, 3), c)[1], 0)

    def forward(layer, inner):
        x = xs[layer]

        def conv_step(r, count):
            for n, acc in enumerate(conv_rows(x, layer, r, count, False)):
                conv[rows((r + n) * TC, TC), :] = acc.reshape(TC, LN)

        def mix(r, count):
            here = pl.ds(pl.multiple_of(r * TC, TC), count * TC)
            v = conv[here, :]
            mean = jnp.sum(v, axis=1, keepdims=True) * (1.0 / CH)
            centred = (v - mean) * lane_ok
            variance = jnp.sum(centred * centred, axis=1, keepdims=True) * (1.0 / CH)
            inverse = lax.rsqrt(variance + epsilon)
            u = centred * inverse
            unit[layer, here, :] = u
            inv[layer, here, :] = jnp.broadcast_to(inverse, (count * TC, LN))
            n = (u * gb[layer, 0:1, :]).astype(bf16)
            normed[layer, here, :] = n
            pre = dot(n, ub[layer], 1, 0)
            e = jnp.exp2(pre * pre * half_log2e)
            t = reciprocal(1.0 + tail_p * jnp.abs(pre))
            poly = tail_c[5] * t + tail_c[4]
            for k in (3, 2, 1, 0):
                poly = poly * t + tail_c[k]
            tail = poly * (t * e)
            cdf = jnp.where(pre >= 0.0, 1.0 - tail, tail)
            h = (pre * cdf).astype(bf16)
            hidden[layer, here, :] = h
            slope[layer, here, :] = cdf + pre * (e * inv_sqrt_two_pi)
            branch = dot(h, db[layer], 1, 1)
            for n in range(count):
                start = (r + n + 3) * ROWV + 24
                value = (x[rows(start, TC), :] + branch[n * TC : n * TC + TC]).astype(bf16).astype(f32)
                if layer == 0:
                    x1[rows(start, TC), :] = value
                else:
                    for j in range(8):
                        stage[pl.ds((r + n) * TC + j, 8, stride=8), :] = value[j * 8 : j * 8 + 8]

        each(inner, conv_step, mix)

    def backward(layer, inner):
        g = gs[layer]

        def mix(r, count):
            here = pl.ds(pl.multiple_of(r * TC, TC), count * TC)
            gr = gradf[here, :].astype(bf16)
            gradb[here, :] = gr
            pg = (dot(gr, db[layer], 1, 0) * slope[layer, here, :]).astype(bf16)
            pregrad[here, :] = pg
            ng = dot(pg, ub[layer], 1, 1)
            u = unit[layer, here, :]
            gain[layer] += jnp.sum((ng * u).reshape(count * 8, 8, LN), axis=0)
            m = ng * gb[layer, 0:1, :]
            mean_m = jnp.sum(m, axis=1, keepdims=True) * (1.0 / CH)
            mean_mu = jnp.sum(m * u, axis=1, keepdims=True) * (1.0 / CH)
            cg = inv[layer, here, :] * (m - mean_m - u * mean_mu)
            cg = cg.astype(bf16).astype(f32)
            for n in range(count):
                g[rows((r + n + 3) * ROWV + 24, TC), :] = cg[n * TC : n * TC + TC]

        each(inner, None, mix)

    def input_grad(layer, inner):
        def step(r, count):
            for n, acc in enumerate(conv_rows(gs[layer], layer, r, count, True)):
                here = rows((r + n) * TC, TC)
                value = (gradf[here, :] + acc.reshape(TC, LN)).astype(bf16).astype(f32)
                if layer == 1:
                    gradf[here, :] = value
                else:
                    for j in range(8):
                        stage[pl.ds((r + n) * TC + j, 8, stride=8), :] = value[j * 8 : j * 8 + 8]

        each(inner, step, None)

    def weight_sums(layer):
        up_sum = dot(normed[layer], pregrad[...], 0, 0)
        down_sum = dot(gradb[...], hidden[layer], 0, 0)
        both = jnp.concatenate([up_sum, down_sum], axis=0).astype(bf16)
        o, k = iota((192, 256), 0), iota((192, 256), 1)
        q = (o * 43691) >> 19
        i = o - q * 12
        pick = (k == ((q >> 1) & 1) * 128 + (q & 1) * 48 + (q >> 2) * 12 + i).astype(f32).astype(bf16)
        ordered = dot(pick, both, 1, 0).astype(bf16)
        for y in range(NY):
            k, n = iota((FF, LN), 0), iota((FF, LN), 1)
            pick = ((k == n + y * 96) & (n < 96)).astype(f32).astype(bf16)
            sblk[layer, y] = dot(ordered, pick, 1, 0).astype(bf16)

    def send_blocks(layer):
        for d in range(1, GROUP):
            ox, oy, device = peer_a(d)
            send(
                sblk.at[layer, oy, pl.ds(pl.multiple_of(ox * 48, 16), 48)],
                rblk.at[layer, d - 1],
                s1_sem.at[layer],
                r1_sem.at[layer],
                device,
            )

    def gather_blocks(layer):
        await_bytes(rblk.at[layer], r1_sem.at[layer])
        total = sblk[layer, py, pl.ds(pl.multiple_of(px * 48, 16), 48)].astype(f32)
        for d in range(1, GROUP):
            total = total + rblk[layer, d - 1].astype(f32)
        sacc[layer * 48 : layer * 48 + 48, :] = total

    def kernel_sums(layer):
        x, g = xs[layer], gs[layer]

        def tap_row(a, _):
            def add(r, acc):
                xa = x[rows((r + a) * ROWV, ROWV), :].reshape(14, 8, LN)
                gr = g[rows((r + 3) * ROWV + 24, TC), :].reshape(8, 8, LN)
                return tuple(acc[b] + jnp.sum(xa[b : b + 8] * gr, axis=0) for b in range(7))

            acc = lax.fori_loop(0, TR, add, tuple(jnp.zeros((8, LN), f32) for _ in range(7)))
            wsum[pl.ds(pl.multiple_of(a * 64, 64), 56), :] = jnp.concatenate(acc, axis=0)
            return 0

        lax.fori_loop(0, 7, tap_row, 0)
        wsum[56:64, :] = gain[layer]
        for a in range(7):
            wa[layer, a * 8 : a * 8 + 8, :] = jnp.sum(wsum[a * 64 : a * 64 + 64, :].reshape(8, 8, LN), axis=1)

    fill_cols(0, x0)
    forward(0, True)
    fill_rows(0, x0)
    forward(0, False)
    pack_halo(1, x1)
    start_halo(1)

    fill_cols(1, x1)
    forward(1, True)
    backward(1, True)
    fill_rows(1, x1)
    forward(1, False)
    backward(1, False)
    pack_halo(2, g1)
    start_halo(2)

    weight_sums(1)
    send_blocks(1)
    kernel_sums(1)
    out_b[...] = stage[:, 0:CH].astype(bf16)
    out_copy = pltpu.make_async_copy(out_b, out, out_sem.at[0])
    out_copy.start()

    fill_cols(2, g1)
    input_grad(1, True)
    backward(0, True)
    fill_rows(2, g1)
    input_grad(1, False)
    backward(0, False)
    pack_halo(3, g0)
    start_halo(3)

    kernel_sums(0)
    send(wa.at[1 - core], wpair, ps_sem, pr_sem, pair)
    weight_sums(0)
    await_bytes(wpair, pr_sem)
    mine_a, mine_z = px * NY + py, zh * (NZC // 2) + zc // 2
    wgroup[mine_a] = (wa[core] + wpair[...]).astype(bf16)
    for d in range(1, GROUP):
        send(wgroup.at[mine_a], wgroup.at[mine_a], as_sem, ar_sem, peer_a(d)[2])
    send_blocks(0)
    gather_blocks(1)

    fill_cols(3, g0)
    input_grad(0, True)
    fill_rows(3, g0)
    input_grad(0, False)

    await_bytes(wgroup.at[pl.ds(0, GROUP - 1)], ar_sem)
    total = wgroup[0].astype(f32)
    for d in range(1, GROUP):
        total = total + wgroup[d].astype(f32)
    wline[mine_z] = total.astype(bf16)
    for d in range(1, 8):
        send(wline.at[mine_z], wline.at[mine_z], zs_sem, zr_sem, peer_b((d // 4) * 8 + (d % 4) * 2)[1])

    gather_blocks(0)
    o, k = iota((LN, LN), 0), iota((LN, LN), 1)
    pick = ((k == (o >> 4) * 12 + (o & 15)) & ((o & 15) < 12)).astype(f32).astype(bf16)
    s2blk[...] = dot(pick, sacc[...].astype(bf16), 1, 1).astype(bf16)
    for d in range(1, GROUP):
        oz, device = peer_b(d)
        send(
            s2blk.at[pl.ds(pl.multiple_of(oz * 16, 16), 16)], r2blk.at[pl.ds((d - 1) * 16, 16)], s2_sem, r2_sem, device
        )

    gimg_b[...] = stage[:, 0:CH].astype(bf16)
    gimg_copy = pltpu.make_async_copy(gimg_b, gimg, out_sem.at[1])
    gimg_copy.start()

    await_bytes(wline.at[pl.ds(0, 7)], zr_sem)
    total = wline[0].astype(f32)
    for d in range(1, 8):
        total = total + wline[d].astype(f32)
    wall[core] = total * (1.0 / 512.0)
    send(wall.at[core], wall.at[core], cs_sem, cr_sem, pair)

    await_bytes(r2blk, r2_sem)
    total = s2blk[pl.ds(pl.multiple_of(zc * 16, 16), 16), :].astype(f32)
    for d in range(1, GROUP):
        total = total + r2blk[(d - 1) * 16 : d * 16, :].astype(f32)
    total = total * (1.0 / 512.0)
    turned = jnp.concatenate([total, jnp.zeros((LN - 16, LN), f32)], axis=0).T
    for layer in range(2):
        o = layer * 48
        gup[:, layer, :] = jnp.where(zh == 0, turned[o : o + 12, 0:12], turned[o + 12 : o + 24, 0:12])
        gdown[:, layer, :] = jnp.where(zh == 0, total[0:12, o + 24 : o + 36], total[0:12, o + 36 : o + 48])

    await_bytes(wall.at[0], cr_sem)
    for layer in range(2):
        for a in range(7):
            gker[a, :, layer, :] = wall[layer, a * 8 : a * 8 + 7, 0:CH]
        ggain[layer : layer + 1, :] = wall[layer, 7:8, 0:CH]

    for e in range(4):
        await_bytes(hsend.at[e], hs_sem.at[e])
    for layer in range(2):
        await_bytes(rblk.at[layer], s1_sem.at[layer])
    await_bytes(r2blk, s2_sem)
    await_bytes(wpair, ps_sem)
    await_bytes(wgroup.at[pl.ds(0, GROUP - 1)], as_sem)
    await_bytes(wline.at[pl.ds(0, 7)], zs_sem)
    await_bytes(wall.at[0], cs_sem)
    out_copy.wait()
    gimg_copy.wait()


def place(*refs):
    for source, target in zip(refs[:6], refs[6:]):
        target[...] = source[...]


def per_device(image, kernels, gains, ups, downs, cot):
    vmem = pltpu.VMEM
    dma = pltpu.SemaphoreType.DMA
    any_spec = pl.BlockSpec(memory_space=pltpu.HBM)
    vmem_spec = pl.BlockSpec(memory_space=pltpu.VMEM)
    outs = pl.pallas_call(
        kernel,
        out_shape=(
            jax.ShapeDtypeStruct((PX, CH), bf16),
            jax.ShapeDtypeStruct((PX, CH), bf16),
            jax.ShapeDtypeStruct((7, 7, 2, CH), f32),
            jax.ShapeDtypeStruct((2, CH), f32),
            jax.ShapeDtypeStruct((12, 2, 12), f32),
            jax.ShapeDtypeStruct((12, 2, 12), f32),
        ),
        in_specs=[any_spec] * 6,
        out_specs=(any_spec, any_spec, vmem_spec, vmem_spec, vmem_spec, vmem_spec),
        scratch_shapes=[
            vmem((PX, CH), bf16),
            vmem((PX, CH), bf16),
            vmem((PX, CH), bf16),
            vmem((PX, CH), bf16),
            vmem((7, 7, 2, CH), f32),
            vmem((2, CH), f32),
            vmem((2, CH, FF), bf16),
            vmem((2, CH, FF), bf16),
            vmem((PADDED, LN), f32),
            vmem((PADDED, LN), f32),
            vmem((PADDED, LN), f32),
            vmem((PADDED, LN), f32),
            vmem((2, 56, 8, LN), f32),
            vmem((2, 8, LN), f32),
            vmem((2, LN, FF), bf16),
            vmem((2, LN, FF), bf16),
            vmem((PX, LN), f32),
            vmem((PX, LN), f32),
            vmem((PX, LN), f32),
            vmem((2, PX, LN), f32),
            vmem((2, PX, LN), f32),
            vmem((2, PX, LN), bf16),
            vmem((2, PX, FF), bf16),
            vmem((2, PX, FF), f32),
            vmem((PX, FF), bf16),
            vmem((PX, LN), bf16),
            vmem((72, LN), f32),
            vmem((72, LN), f32),
            vmem((64, LN), f32),
            vmem((4, HALO, LN), bf16),
            vmem((4, HALO, LN), bf16),
            vmem((2, 8, LN), f32),
            vmem((7 * 64, LN), f32),
            vmem((2, NY, 192, LN), bf16),
            vmem((2, GROUP - 1, 48, LN), bf16),
            vmem((LN, LN), f32),
            vmem((LN, LN), bf16),
            vmem(((GROUP - 1) * 16, LN), bf16),
            vmem((2, 64, LN), f32),
            vmem((64, LN), f32),
            vmem((GROUP, 64, LN), bf16),
            vmem((8, 64, LN), bf16),
            vmem((2, 64, LN), f32),
            dma((6,)),
            dma((2,)),
            dma((4,)),
            dma((4,)),
            dma((4,)),
            dma((2,)),
            dma((2,)),
        ]
        + [dma] * 10,
        compiler_params=pltpu.CompilerParams(
            collective_id=0, has_side_effects=True, vmem_limit_bytes=63 * 1024 * 1024
        ),
        cost_estimate=pl.CostEstimate(flops=2000000000, bytes_accessed=2000000, transcendentals=1600000),
    )(
        image.reshape(PX, CH), kernels.transpose(1, 2, 0, 3), gains, ups, downs.transpose(0, 2, 1), cot.reshape(PX, CH)
    )
    outs = pl.pallas_call(
        place,
        out_shape=tuple(jax.ShapeDtypeStruct(o.shape, o.dtype) for o in outs),
        in_specs=[vmem_spec] * 6,
        out_specs=(vmem_spec,) * 6,
    )(*outs)
    return (
        outs[0].reshape(TR, TC, CH),
        outs[1].reshape(TR, TC, CH),
        outs[2].transpose(2, 0, 1, 3),
        outs[3],
        outs[4].transpose(1, 0, 2),
        outs[5].transpose(1, 0, 2),
    )


def solution(mesh):
    placed = (P("row", "col", None), P(), P(), P(), P(), P("row", "col", None))
    return jax.shard_map(
        per_device,
        mesh=mesh,
        in_specs=placed,
        out_specs=(
            P("row", "col", None),
            P("row", "col", None),
            P(),
            P(),
            P(None, "row", "col"),
            P(None, "col", "row"),
        ),
        check_vma=False,
    )
```

```python
import functools
import math

import jax
import jax.numpy as jnp
from jax import lax
from jax.experimental import pallas as pl
from jax.experimental.pallas import tpu as pltpu
from jax.sharding import PartitionSpec as P

f32 = jnp.float32
bf16 = jnp.bfloat16
MESH = pl.DeviceIdType.MESH

epsilon = 1e-06
inv_sqrt_two_pi = 0.3989422804014327
half_log2e = -0.7213475204444817
tail_p = 0.275
tail_c = (
    0.11780924948816489,
    0.04211150374007564,
    0.33393224058082305,
    -0.33099335173379324,
    0.45199869046687746,
    -0.11485832782346941,
)

NX, NZH, NY, NZC = 4, 2, 4, 8
TR, TC, CH, FF, LN = 16, 64, 96, 384, 128
PX = TR * TC
ROWV = 14 * 8
PADDED = 22 * ROWV
HALO = 544
GROUP = 16


def reciprocal(d):
    return pltpu.reciprocal(d, approx=True)


def dot(a, b, ca, cb):
    return lax.dot_general(a, b, (((ca,), (cb,)), ((), ())), preferred_element_type=f32)


def iota(shape, dim):
    return lax.broadcasted_iota(jnp.int32, shape, dim)


def kernel(
    image, kernels, gains, ups, downs, cot,
    out, gimg, gker, ggain, gup, gdown,
    img_in, cot_in, out_b, gimg_b, k_in, g_in, u_in, d_in,
    x0, x1, g0, g1, kb, gb, ub, db, stage, gradf, conv, unit, inv, normed, hidden, slope, pregrad, gradb,
    lf, rf, corner, hsend, hrecv, gain, wsum, sblk, rblk, sacc, s2blk, r2blk, wa, wpair, wgroup, wline, wall,
    in_sem, out_sem, hs_sem, hc_sem, hr_sem, s1_sem, r1_sem, s2_sem, r2_sem, ps_sem, pr_sem, as_sem, ar_sem,
    zs_sem, zr_sem, cs_sem, cr_sem,
):
    xs = (x0, x1)
    gs = (g0, g1)
    ri = lax.axis_index("row")
    ci = lax.axis_index("col")
    zh, px = ri // NX, ri % NX
    py, zc = ci // NZC, ci % NZC
    core = ci % 2
    nrow, ncol = NX * NZH, NY * NZC

    def peer_a(d):
        ox = (px + d // NY) % NX
        oy = (py + d % NY) % NY
        return ox, oy, (zh * NX + ox, oy * NZC + zc)

    def peer_b(d):
        oh = (zh + d // NZC) % NZH
        oz = (zc + d % NZC) % NZC
        return oz, (oh * NX + px, py * NZC + oz)

    def send(src, dst, send_sem, recv_sem, device):
        pltpu.make_async_remote_copy(
            src_ref=src, dst_ref=dst, send_sem=send_sem, recv_sem=recv_sem, device_id=device, device_id_type=MESH
        ).start()

    def await_bytes(ref, sem):
        pltpu.make_async_copy(ref, ref, sem).wait()

    up_r, dn_r = (ri + nrow - 1) % nrow, (ri + 1) % nrow
    lt_c, rt_c = (ci + ncol - 1) % ncol, (ci + 1) % ncol
    pair = (ri, ci + 1 - 2 * core)

    loads = [
        pltpu.make_async_copy(src, dst, in_sem.at[i])
        for i, (src, dst) in enumerate(
            ((image, img_in), (kernels, k_in), (gains, g_in), (ups, u_in), (downs, d_in), (cot, cot_in))
        )
    ]
    for load in loads:
        load.start()

    barrier = pltpu.get_barrier_semaphore()
    near = [(up_r, ci), (dn_r, ci), (ri, lt_c), (ri, rt_c), (up_r, lt_c), (up_r, rt_c), (dn_r, lt_c), (dn_r, rt_c)]
    everyone = near + [peer_a(d)[2] for d in range(1, GROUP)] + [peer_b(d)[1] for d in range(1, GROUP)]
    for device in everyone:
        pl.semaphore_signal(barrier, inc=1, device_id=device, device_id_type=MESH)

    def rows(start, size):
        return pl.ds(pl.multiple_of(start, 8), size)

    def pack_halo(e, x):
        for q in range(3):
            left, right = (3 + q) * 8, (8 + q) * 8 + 7
            hsend[e, q * 16 : q * 16 + 16] = x[pl.ds(3 * ROWV + left, TR, stride=ROWV), :].astype(bf16)
            hsend[e, 48 + q * 16 : 64 + q * 16] = x[pl.ds(3 * ROWV + right, TR, stride=ROWV), :].astype(bf16)
            top, bottom = (3 + q) * ROWV + 24, (16 + q) * ROWV + 24
            hsend[e, 96 + q * 64 : 160 + q * 64] = x[top : top + 64, :].astype(bf16)
            hsend[e, 288 + q * 64 : 352 + q * 64] = x[bottom : bottom + 64, :].astype(bf16)
            for c, start in enumerate(
                (3 * ROWV + left, 3 * ROWV + right, 16 * ROWV + left, 16 * ROWV + right)
            ):
                corner[c * 16 + q * 4 : c * 16 + q * 4 + 3, :] = x[pl.ds(start, 3, stride=ROWV), :]
        hsend[e, 480:544] = corner[...].astype(bf16)

    def start_halo(e):
        for source, size, target, sem, device in (
            (0, 48, 48, hc_sem, (ri, lt_c)),
            (48, 48, 0, hc_sem, (ri, rt_c)),
            (96, 192, 288, hr_sem, (up_r, ci)),
            (288, 192, 96, hr_sem, (dn_r, ci)),
            (480, 16, 528, hr_sem, (up_r, lt_c)),
            (496, 16, 512, hr_sem, (up_r, rt_c)),
            (512, 16, 496, hr_sem, (dn_r, lt_c)),
            (528, 16, 480, hr_sem, (dn_r, rt_c)),
        ):
            send(hsend.at[e, pl.ds(source, size)], hrecv.at[e, pl.ds(target, size)], hs_sem.at[e], sem.at[e], device)

    m_up = jnp.where(ri == 0, 0.0, 1.0).astype(f32)
    m_dn = jnp.where(ri == nrow - 1, 0.0, 1.0).astype(f32)
    m_lt = jnp.where(ci == 0, 0.0, 1.0).astype(f32)
    m_rt = jnp.where(ci == ncol - 1, 0.0, 1.0).astype(f32)
    first = iota((8, LN), 0) == 0
    last = iota((8, LN), 0) == 7

    def extend_row(x, r):
        base = r * ROWV
        for q in range(3):
            v = x[rows(base + (8 + q) * 8, 8), :]
            edge = jnp.broadcast_to(lf[pl.ds(q * 24 + r, 1), :], (8, LN))
            x[rows(base + q * 8, 8), :] = jnp.where(first, edge, pltpu.roll(v, 1, 0))
            v = x[rows(base + (3 + q) * 8, 8), :]
            edge = jnp.broadcast_to(rf[pl.ds(q * 24 + r, 1), :], (8, LN))
            x[rows(base + (11 + q) * 8, 8), :] = jnp.where(last, edge, pltpu.roll(v, 7, 0))

    def fill_cols(e, x):
        await_bytes(hrecv.at[e, pl.ds(0, 96)], hc_sem.at[e])
        for q in range(3):
            lf[q * 24 + 3 : q * 24 + 19, :] = hrecv[e, q * 16 : q * 16 + 16].astype(f32) * m_lt
            rf[q * 24 + 3 : q * 24 + 19, :] = hrecv[e, 48 + q * 16 : 64 + q * 16].astype(f32) * m_rt

        def step(i, _):
            extend_row(x, 3 + 2 * i)
            extend_row(x, 4 + 2 * i)
            return 0

        lax.fori_loop(0, TR // 2, step, 0)

    def fill_rows(e, x):
        await_bytes(hrecv.at[e, pl.ds(96, 448)], hr_sem.at[e])
        corners = hrecv[e, 480:544].astype(f32)
        for q in range(3):
            x[q * ROWV + 24 : q * ROWV + 88, :] = hrecv[e, 96 + q * 64 : 160 + q * 64].astype(f32) * m_up
            x[(19 + q) * ROWV + 24 : (19 + q) * ROWV + 88, :] = (
                hrecv[e, 288 + q * 64 : 352 + q * 64].astype(f32) * m_dn
            )
            o = q * 24
            for c, (ref, m, at) in enumerate(
                ((lf, m_lt * m_up, o), (rf, m_rt * m_up, o), (lf, m_lt * m_dn, o + 19), (rf, m_rt * m_dn, o + 19))
            ):
                ref[at : at + 3, :] = corners[c * 16 + q * 4 : c * 16 + q * 4 + 3] * m

        def step(i, _):
            extend_row(x, i)
            extend_row(x, i + 19)
            return 0

        lax.fori_loop(0, 3, step, 0)

    def conv_rows(x, layer, r, count, flip):
        accs = [None] * count
        for a in range(6 + count):
            xa = x[rows((r + a) * ROWV, ROWV), :].reshape(14, 8, LN)
            for b in range(7):
                for n in range(count):
                    if 0 <= a - n < 7:
                        tap = (6 - a + n) * 8 + 6 - b if flip else (a - n) * 8 + b
                        term = xa[b : b + 8] * kb[layer, tap][None]
                        accs[n] = term if accs[n] is None else accs[n] + term
        return accs

    stage[...] = jnp.zeros_like(stage)
    corner[...] = jnp.zeros_like(corner)
    loads[0].wait()
    stage[:, 0:CH] = img_in[...].astype(f32)

    def spread(r, _):
        for j in range(8):
            x0[rows((r + 3) * ROWV + (3 + j) * 8, 8), :] = stage[pl.ds(r * TC + j, 8, stride=8), :]
        return 0

    lax.fori_loop(0, TR, spread, 0)
    pack_halo(0, x0)
    pl.semaphore_wait(barrier, len(everyone))
    start_halo(0)

    gb[...] = jnp.zeros_like(gb)
    ub[...] = jnp.zeros_like(ub)
    db[...] = jnp.zeros_like(db)
    kb[...] = jnp.zeros_like(kb)
    gain[...] = jnp.zeros_like(gain)
    sacc[...] = jnp.zeros_like(sacc)
    wsum[...] = jnp.zeros_like(wsum)
    wa[...] = jnp.zeros_like(wa)
    for load in loads[1:]:
        load.wait()
    for layer in range(2):
        gb[layer, 0:1, 0:CH] = g_in[layer : layer + 1, :]
        ub[layer, 0:CH, :] = u_in[layer]
        db[layer, 0:CH, :] = d_in[layer]
        for a in range(7):
            for b in range(7):
                kb[layer, a * 8 + b, :, 0:CH] = jnp.broadcast_to(k_in[a, b, layer : layer + 1, :], (8, CH))
    stage[:, 0:CH] = cot_in[...].astype(f32)

    def spread_cot(r, _):
        for j in range(8):
            gradf[rows(r * TC + j * 8, 8), :] = stage[pl.ds(r * TC + j, 8, stride=8), :]
        return 0

    lax.fori_loop(0, TR, spread_cot, 0)
    lane_ok = jnp.where(iota((8, LN), 1) < CH, 1.0, 0.0).astype(f32)[0:1]

    INNER = ((3, 10),)
    OUTER = ((0, 3), (13, 3))

    def part(inner, conv_step, mix_step):
        if conv_step is not None:
            if inner:
                lax.fori_loop(0, 5, lambda i, c: (conv_step(3 + 2 * i, 2), c)[1], 0)
            else:
                lax.fori_loop(0, 2, lambda i, c: (conv_step(13 * i, 3), c)[1], 0)
        if mix_step is not None:
            mix_step(INNER if inner else OUTER)

    def take(ref, spans):
        return jnp.concatenate([ref[r * TC : (r + n) * TC, :] for r, n in spans], axis=0)

    def put(ref, spans, value):
        at = 0
        for r, n in spans:
            ref[r * TC : (r + n) * TC, :] = value[at : at + n * TC]
            at += n * TC

    def listed(spans):
        return [r + k for r, n in spans for k in range(n)]

    def forward(layer, inner):
        x = xs[layer]

        def conv_step(r, count):
            for n, acc in enumerate(conv_rows(x, layer, r, count, False)):
                conv[rows((r + n) * TC, TC), :] = acc.reshape(TC, LN)

        def mix(spans):
            v = take(conv, spans)
            mean = jnp.sum(v, axis=1, keepdims=True) * (1.0 / CH)
            centred = (v - mean) * lane_ok
            variance = jnp.sum(centred * centred, axis=1, keepdims=True) * (1.0 / CH)
            inverse = lax.rsqrt(variance + epsilon)
            u = centred * inverse
            put(unit.at[layer], spans, u)
            put(inv.at[layer], spans, jnp.broadcast_to(inverse, u.shape))
            n = (u * gb[layer, 0:1, :]).astype(bf16)
            put(normed.at[layer], spans, n)
            pre = dot(n, ub[layer], 1, 0)
            e = jnp.exp2(pre * pre * half_log2e)
            t = reciprocal(1.0 + tail_p * jnp.abs(pre))
            poly = tail_c[5] * t + tail_c[4]
            for k in (3, 2, 1, 0):
                poly = poly * t + tail_c[k]
            tail = poly * (t * e)
            cdf = jnp.where(pre >= 0.0, 1.0 - tail, tail)
            h = (pre * cdf).astype(bf16)
            put(hidden.at[layer], spans, h)
            put(slope.at[layer], spans, cdf + pre * (e * inv_sqrt_two_pi))
            branch = dot(h, db[layer], 1, 1)
            for n, r in enumerate(listed(spans)):
                start = (r + 3) * ROWV + 24
                value = (x[start : start + TC, :] + branch[n * TC : n * TC + TC]).astype(bf16).astype(f32)
                if layer == 0:
                    x1[start : start + TC, :] = value
                else:
                    for j in range(8):
                        stage[pl.ds(r * TC + j, 8, stride=8), :] = value[j * 8 : j * 8 + 8]

        part(inner, conv_step, mix)

    def backward(layer, inner):
        g = gs[layer]

        def mix(spans):
            gr = take(gradf, spans).astype(bf16)
            put(gradb, spans, gr)
            pg = (dot(gr, db[layer], 1, 0) * take(slope.at[layer], spans)).astype(bf16)
            put(pregrad, spans, pg)
            ng = dot(pg, ub[layer], 1, 1)
            u = take(unit.at[layer], spans)
            gain[layer] += jnp.sum((ng * u).reshape(u.shape[0] // 8, 8, LN), axis=0)
            m = ng * gb[layer, 0:1, :]
            mean_m = jnp.sum(m, axis=1, keepdims=True) * (1.0 / CH)
            mean_mu = jnp.sum(m * u, axis=1, keepdims=True) * (1.0 / CH)
            cg = take(inv.at[layer], spans) * (m - mean_m - u * mean_mu)
            cg = cg.astype(bf16).astype(f32)
            for n, r in enumerate(listed(spans)):
                start = (r + 3) * ROWV + 24
                g[start : start + TC, :] = cg[n * TC : n * TC + TC]

        part(inner, None, mix)

    def input_grad(layer, inner):
        def step(r, count):
            for n, acc in enumerate(conv_rows(gs[layer], layer, r, count, True)):
                here = rows((r + n) * TC, TC)
                value = (gradf[here, :] + acc.reshape(TC, LN)).astype(bf16).astype(f32)
                if layer == 1:
                    gradf[here, :] = value
                else:
                    for j in range(8):
                        stage[pl.ds((r + n) * TC + j, 8, stride=8), :] = value[j * 8 : j * 8 + 8]

        part(inner, step, None)

    def weight_sums(layer):
        up_sum = dot(normed[layer], pregrad[...], 0, 0)
        down_sum = dot(gradb[...], hidden[layer], 0, 0)
        both = jnp.concatenate([up_sum, down_sum], axis=0).astype(bf16)
        o, k = iota((192, 256), 0), iota((192, 256), 1)
        q = (o * 43691) >> 19
        i = o - q * 12
        pick = (k == ((q >> 1) & 1) * 128 + (q & 1) * 48 + (q >> 2) * 12 + i).astype(f32).astype(bf16)
        ordered = dot(pick, both, 1, 0).astype(bf16)
        for y in range(NY):
            k, n = iota((FF, LN), 0), iota((FF, LN), 1)
            pick = ((k == n + y * 96) & (n < 96)).astype(f32).astype(bf16)
            sblk[layer, y] = dot(ordered, pick, 1, 0).astype(bf16)

    def send_blocks(layer):
        for d in range(1, GROUP):
            ox, oy, device = peer_a(d)
            send(
                sblk.at[layer, oy, pl.ds(pl.multiple_of(ox * 48, 16), 48)],
                rblk.at[layer, d - 1],
                s1_sem.at[layer],
                r1_sem.at[layer],
                device,
            )

    def gather_blocks(layer):
        await_bytes(rblk.at[layer], r1_sem.at[layer])
        total = sblk[layer, py, pl.ds(pl.multiple_of(px * 48, 16), 48)].astype(f32)
        for d in range(1, GROUP):
            total = total + rblk[layer, d - 1].astype(f32)
        sacc[layer * 48 : layer * 48 + 48, :] = total

    def kernel_sums(layer, inner):
        x, g = xs[layer], gs[layer]

        def products(r, a):
            xa = x[rows((r + a) * ROWV, ROWV), :].reshape(14, 8, LN)
            gr = g[rows((r + 3) * ROWV + 24, TC), :].reshape(8, 8, LN)
            return tuple(jnp.sum(xa[b : b + 8] * gr, axis=0) for b in range(7))

        def tap_row(a, _):
            here = pl.ds(pl.multiple_of(a * 64, 64), 56)
            if inner:
                zero = tuple(jnp.zeros((8, LN), f32) for _ in range(7))
                acc = lax.fori_loop(
                    0, 2, lambda i, acc: fold(acc, [products(3 + 5 * i + n, a) for n in range(5)]), zero
                )
                wsum[here, :] = jnp.concatenate(acc, axis=0)
            else:
                acc = tuple(wsum[pl.ds(pl.multiple_of(a * 64 + b * 8, 8), 8), :] for b in range(7))
                acc = fold(acc, [products(r, a) for r in listed(OUTER)])
                wsum[here, :] = jnp.concatenate(acc, axis=0)
            return 0

        def fold(acc, terms):
            for term in terms:
                acc = tuple(p + q for p, q in zip(acc, term))
            return acc

        lax.fori_loop(0, 7, tap_row, 0)
        if not inner:
            wsum[56:64, :] = gain[layer]
            for a in range(7):
                wa[layer, a * 8 : a * 8 + 8, :] = jnp.sum(wsum[a * 64 : a * 64 + 64, :].reshape(8, 8, LN), axis=1)

    fill_cols(0, x0)
    forward(0, True)
    fill_rows(0, x0)
    forward(0, False)
    pack_halo(1, x1)
    start_halo(1)

    fill_cols(1, x1)
    forward(1, True)
    backward(1, True)
    fill_rows(1, x1)
    forward(1, False)
    backward(1, False)
    pack_halo(2, g1)
    start_halo(2)

    weight_sums(1)
    send_blocks(1)
    kernel_sums(1, True)
    kernel_sums(1, False)
    out_b[...] = stage[:, 0:CH].astype(bf16)
    out_copy = pltpu.make_async_copy(out_b, out, out_sem.at[0])
    out_copy.start()

    fill_cols(2, g1)
    input_grad(1, True)
    backward(0, True)
    kernel_sums(0, True)
    fill_rows(2, g1)
    input_grad(1, False)
    backward(0, False)
    pack_halo(3, g0)
    start_halo(3)

    kernel_sums(0, False)
    send(wa.at[1 - core], wpair, ps_sem, pr_sem, pair)
    weight_sums(0)
    await_bytes(wpair, pr_sem)
    mine_a, mine_z = px * NY + py, zh * (NZC // 2) + zc // 2
    wgroup[mine_a] = (wa[core] + wpair[...]).astype(bf16)
    for d in range(1, GROUP):
        send(wgroup.at[mine_a], wgroup.at[mine_a], as_sem, ar_sem, peer_a(d)[2])
    send_blocks(0)
    gather_blocks(1)

    fill_cols(3, g0)
    input_grad(0, True)
    fill_rows(3, g0)
    input_grad(0, False)

    await_bytes(wgroup.at[pl.ds(0, GROUP - 1)], ar_sem)
    total = wgroup[0].astype(f32)
    for d in range(1, GROUP):
        total = total + wgroup[d].astype(f32)
    wline[mine_z] = total.astype(bf16)
    for d in range(1, 8):
        send(wline.at[mine_z], wline.at[mine_z], zs_sem, zr_sem, peer_b((d // 4) * 8 + (d % 4) * 2)[1])

    gather_blocks(0)
    o, k = iota((LN, LN), 0), iota((LN, LN), 1)
    pick = ((k == (o >> 4) * 12 + (o & 15)) & ((o & 15) < 12)).astype(f32).astype(bf16)
    s2blk[...] = dot(pick, sacc[...].astype(bf16), 1, 1).astype(bf16)
    for d in range(1, GROUP):
        oz, device = peer_b(d)
        send(
            s2blk.at[pl.ds(pl.multiple_of(oz * 16, 16), 16)], r2blk.at[pl.ds((d - 1) * 16, 16)], s2_sem, r2_sem, device
        )

    gimg_b[...] = stage[:, 0:CH].astype(bf16)
    gimg_copy = pltpu.make_async_copy(gimg_b, gimg, out_sem.at[1])
    gimg_copy.start()

    await_bytes(wline.at[pl.ds(0, 7)], zr_sem)
    total = wline[0].astype(f32)
    for d in range(1, 8):
        total = total + wline[d].astype(f32)
    wall[core] = total * (1.0 / 512.0)
    send(wall.at[core], wall.at[core], cs_sem, cr_sem, pair)

    await_bytes(r2blk, r2_sem)
    total = s2blk[pl.ds(pl.multiple_of(zc * 16, 16), 16), :].astype(f32)
    for d in range(1, GROUP):
        total = total + r2blk[(d - 1) * 16 : d * 16, :].astype(f32)
    total = total * (1.0 / 512.0)
    turned = jnp.concatenate([total, jnp.zeros((LN - 16, LN), f32)], axis=0).T
    for layer in range(2):
        o = layer * 48
        gup[:, layer, :] = jnp.where(zh == 0, turned[o : o + 12, 0:12], turned[o + 12 : o + 24, 0:12])
        gdown[:, layer, :] = jnp.where(zh == 0, total[0:12, o + 24 : o + 36], total[0:12, o + 36 : o + 48])

    await_bytes(wall.at[0], cr_sem)
    for layer in range(2):
        for a in range(7):
            gker[a, :, layer, :] = wall[layer, a * 8 : a * 8 + 7, 0:CH]
        ggain[layer : layer + 1, :] = wall[layer, 7:8, 0:CH]

    for e in range(4):
        await_bytes(hsend.at[e], hs_sem.at[e])
    for layer in range(2):
        await_bytes(rblk.at[layer], s1_sem.at[layer])
    await_bytes(r2blk, s2_sem)
    await_bytes(wpair, ps_sem)
    await_bytes(wgroup.at[pl.ds(0, GROUP - 1)], as_sem)
    await_bytes(wline.at[pl.ds(0, 7)], zs_sem)
    await_bytes(wall.at[0], cs_sem)
    out_copy.wait()
    gimg_copy.wait()


def place(*refs):
    for source, target in zip(refs[:6], refs[6:]):
        target[...] = source[...]


def per_device(image, kernels, gains, ups, downs, cot):
    vmem = pltpu.VMEM
    dma = pltpu.SemaphoreType.DMA
    any_spec = pl.BlockSpec(memory_space=pltpu.HBM)
    vmem_spec = pl.BlockSpec(memory_space=pltpu.VMEM)
    outs = pl.pallas_call(
        kernel,
        out_shape=(
            jax.ShapeDtypeStruct((PX, CH), bf16),
            jax.ShapeDtypeStruct((PX, CH), bf16),
            jax.ShapeDtypeStruct((7, 7, 2, CH), f32),
            jax.ShapeDtypeStruct((2, CH), f32),
            jax.ShapeDtypeStruct((12, 2, 12), f32),
            jax.ShapeDtypeStruct((12, 2, 12), f32),
        ),
        in_specs=[any_spec] * 6,
        out_specs=(any_spec, any_spec, vmem_spec, vmem_spec, vmem_spec, vmem_spec),
        scratch_shapes=[
            vmem((PX, CH), bf16),
            vmem((PX, CH), bf16),
            vmem((PX, CH), bf16),
            vmem((PX, CH), bf16),
            vmem((7, 7, 2, CH), f32),
            vmem((2, CH), f32),
            vmem((2, CH, FF), bf16),
            vmem((2, CH, FF), bf16),
            vmem((PADDED, LN), f32),
            vmem((PADDED, LN), f32),
            vmem((PADDED, LN), f32),
            vmem((PADDED, LN), f32),
            vmem((2, 56, 8, LN), f32),
            vmem((2, 8, LN), f32),
            vmem((2, LN, FF), bf16),
            vmem((2, LN, FF), bf16),
            vmem((PX, LN), f32),
            vmem((PX, LN), f32),
            vmem((PX, LN), f32),
            vmem((2, PX, LN), f32),
            vmem((2, PX, LN), f32),
            vmem((2, PX, LN), bf16),
            vmem((2, PX, FF), bf16),
            vmem((2, PX, FF), f32),
            vmem((PX, FF), bf16),
            vmem((PX, LN), bf16),
            vmem((72, LN), f32),
            vmem((72, LN), f32),
            vmem((64, LN), f32),
            vmem((4, HALO, LN), bf16),
            vmem((4, HALO, LN), bf16),
            vmem((2, 8, LN), f32),
            vmem((7 * 64, LN), f32),
            vmem((2, NY, 192, LN), bf16),
            vmem((2, GROUP - 1, 48, LN), bf16),
            vmem((LN, LN), f32),
            vmem((LN, LN), bf16),
            vmem(((GROUP - 1) * 16, LN), bf16),
            vmem((2, 64, LN), f32),
            vmem((64, LN), f32),
            vmem((GROUP, 64, LN), bf16),
            vmem((8, 64, LN), bf16),
            vmem((2, 64, LN), f32),
            dma((6,)),
            dma((2,)),
            dma((4,)),
            dma((4,)),
            dma((4,)),
            dma((2,)),
            dma((2,)),
        ]
        + [dma] * 10,
        compiler_params=pltpu.CompilerParams(
            collective_id=0, has_side_effects=True, vmem_limit_bytes=63 * 1024 * 1024
        ),
        cost_estimate=pl.CostEstimate(flops=2000000000, bytes_accessed=2000000, transcendentals=1600000),
    )(
        image.reshape(PX, CH), kernels.transpose(1, 2, 0, 3), gains, ups, downs.transpose(0, 2, 1), cot.reshape(PX, CH)
    )
    outs = pl.pallas_call(
        place,
        out_shape=tuple(jax.ShapeDtypeStruct(o.shape, o.dtype) for o in outs),
        in_specs=[vmem_spec] * 6,
        out_specs=(vmem_spec,) * 6,
    )(*outs)
    return (
        outs[0].reshape(TR, TC, CH),
        outs[1].reshape(TR, TC, CH),
        outs[2].transpose(2, 0, 1, 3),
        outs[3],
        outs[4].transpose(1, 0, 2),
        outs[5].transpose(1, 0, 2),
    )


def solution(mesh):
    placed = (P("row", "col", None), P(), P(), P(), P(), P("row", "col", None))
    return jax.shard_map(
        per_device,
        mesh=mesh,
        in_specs=placed,
        out_specs=(
            P("row", "col", None),
            P("row", "col", None),
            P(),
            P(),
            P(None, "row", "col"),
            P(None, "col", "row"),
        ),
        check_vma=False,
    )
```

```python
import functools
import math

import jax
import jax.numpy as jnp
from jax import lax
from jax.experimental import pallas as pl
from jax.experimental.pallas import tpu as pltpu
from jax.sharding import PartitionSpec as P

f32 = jnp.float32
bf16 = jnp.bfloat16
MESH = pl.DeviceIdType.MESH

epsilon = 1e-06
inv_sqrt_two_pi = 0.3989422804014327
half_log2e = -0.7213475204444817
tail_p = 0.275
tail_c = (
    0.11780924948816489,
    0.04211150374007564,
    0.33393224058082305,
    -0.33099335173379324,
    0.45199869046687746,
    -0.11485832782346941,
)

NX, NZH, NY, NZC = 4, 2, 4, 8
TR, TC, CH, FF, LN = 16, 64, 96, 384, 128
PX = TR * TC
ROWV = 14 * 8
PADDED = 22 * ROWV
HALO = 544
GROUP = 16


def reciprocal(d):
    return pltpu.reciprocal(d, approx=True)


def dot(a, b, ca, cb):
    return lax.dot_general(a, b, (((ca,), (cb,)), ((), ())), preferred_element_type=f32)


def iota(shape, dim):
    return lax.broadcasted_iota(jnp.int32, shape, dim)


def kernel(
    image, kernels, gains, ups, downs, cot,
    out, gimg, gker, ggain, gup, gdown,
    img_in, cot_in, out_b, gimg_b, k_in, g_in, u_in, d_in,
    x0, x1, g0, g1, kb, gb, ub, db, stage, gradf, conv, unit, inv, normed, hidden, slope, pregrad, gradb,
    lf, rf, corner, hsend, hrecv, gain, pick_rows, pick_cols, pick_units, wsum, sblk, rblk, sacc, s2blk, r2blk, wa, wpair, wgroup, wline, wall,
    in_sem, out_sem, hs_sem, hc_sem, hr_sem, s1_sem, r1_sem, s2_sem, r2_sem, ps_sem, pr_sem, as_sem, ar_sem,
    zs_sem, zr_sem, cs_sem, cr_sem,
):
    xs = (x0, x1)
    gs = (g0, g1)
    ri = lax.axis_index("row")
    ci = lax.axis_index("col")
    zh, px = ri // NX, ri % NX
    py, zc = ci // NZC, ci % NZC
    core = ci % 2
    nrow, ncol = NX * NZH, NY * NZC

    def peer_a(d):
        ox = (px + d // NY) % NX
        oy = (py + d % NY) % NY
        return ox, oy, (zh * NX + ox, oy * NZC + zc)

    def peer_b(d):
        oh = (zh + d // NZC) % NZH
        oz = (zc + d % NZC) % NZC
        return oz, (oh * NX + px, py * NZC + oz)

    def send(src, dst, send_sem, recv_sem, device):
        pltpu.make_async_remote_copy(
            src_ref=src, dst_ref=dst, send_sem=send_sem, recv_sem=recv_sem, device_id=device, device_id_type=MESH
        ).start()

    def await_bytes(ref, sem):
        pltpu.make_async_copy(ref, ref, sem).wait()

    up_r, dn_r = (ri + nrow - 1) % nrow, (ri + 1) % nrow
    lt_c, rt_c = (ci + ncol - 1) % ncol, (ci + 1) % ncol
    pair = (ri, ci + 1 - 2 * core)

    loads = [
        pltpu.make_async_copy(src, dst, in_sem.at[i])
        for i, (src, dst) in enumerate(
            ((image, img_in), (kernels, k_in), (gains, g_in), (ups, u_in), (downs, d_in), (cot, cot_in))
        )
    ]
    for load in loads:
        load.start()

    barrier = pltpu.get_barrier_semaphore()
    near = [(up_r, ci), (dn_r, ci), (ri, lt_c), (ri, rt_c), (up_r, lt_c), (up_r, rt_c), (dn_r, lt_c), (dn_r, rt_c)]
    everyone = near + [peer_a(d)[2] for d in range(1, GROUP)] + [peer_b(d)[1] for d in range(1, GROUP)]
    for device in everyone:
        pl.semaphore_signal(barrier, inc=1, device_id=device, device_id_type=MESH)

    def rows(start, size):
        return pl.ds(pl.multiple_of(start, 8), size)

    def pack_halo(e, x):
        for q in range(3):
            left, right = (3 + q) * 8, (8 + q) * 8 + 7
            hsend[e, q * 16 : q * 16 + 16] = x[pl.ds(3 * ROWV + left, TR, stride=ROWV), :].astype(bf16)
            hsend[e, 48 + q * 16 : 64 + q * 16] = x[pl.ds(3 * ROWV + right, TR, stride=ROWV), :].astype(bf16)
            top, bottom = (3 + q) * ROWV + 24, (16 + q) * ROWV + 24
            hsend[e, 96 + q * 64 : 160 + q * 64] = x[top : top + 64, :].astype(bf16)
            hsend[e, 288 + q * 64 : 352 + q * 64] = x[bottom : bottom + 64, :].astype(bf16)
            for c, start in enumerate(
                (3 * ROWV + left, 3 * ROWV + right, 16 * ROWV + left, 16 * ROWV + right)
            ):
                corner[c * 16 + q * 4 : c * 16 + q * 4 + 3, :] = x[pl.ds(start, 3, stride=ROWV), :]
        hsend[e, 480:544] = corner[...].astype(bf16)

    def start_halo(e):
        for source, size, target, sem, device in (
            (0, 48, 48, hc_sem, (ri, lt_c)),
            (48, 48, 0, hc_sem, (ri, rt_c)),
            (96, 192, 288, hr_sem, (up_r, ci)),
            (288, 192, 96, hr_sem, (dn_r, ci)),
            (480, 16, 528, hr_sem, (up_r, lt_c)),
            (496, 16, 512, hr_sem, (up_r, rt_c)),
            (512, 16, 496, hr_sem, (dn_r, lt_c)),
            (528, 16, 480, hr_sem, (dn_r, rt_c)),
        ):
            send(hsend.at[e, pl.ds(source, size)], hrecv.at[e, pl.ds(target, size)], hs_sem.at[e], sem.at[e], device)

    m_up = jnp.where(ri == 0, 0.0, 1.0).astype(f32)
    m_dn = jnp.where(ri == nrow - 1, 0.0, 1.0).astype(f32)
    m_lt = jnp.where(ci == 0, 0.0, 1.0).astype(f32)
    m_rt = jnp.where(ci == ncol - 1, 0.0, 1.0).astype(f32)
    first = iota((8, LN), 0) == 0
    last = iota((8, LN), 0) == 7

    def extend_row(x, r):
        base = r * ROWV
        for q in range(3):
            v = x[rows(base + (8 + q) * 8, 8), :]
            edge = jnp.broadcast_to(lf[pl.ds(q * 24 + r, 1), :], (8, LN))
            x[rows(base + q * 8, 8), :] = jnp.where(first, edge, pltpu.roll(v, 1, 0))
            v = x[rows(base + (3 + q) * 8, 8), :]
            edge = jnp.broadcast_to(rf[pl.ds(q * 24 + r, 1), :], (8, LN))
            x[rows(base + (11 + q) * 8, 8), :] = jnp.where(last, edge, pltpu.roll(v, 7, 0))

    def fill_cols(e, x):
        await_bytes(hrecv.at[e, pl.ds(0, 96)], hc_sem.at[e])
        for q in range(3):
            lf[q * 24 + 3 : q * 24 + 19, :] = hrecv[e, q * 16 : q * 16 + 16].astype(f32) * m_lt
            rf[q * 24 + 3 : q * 24 + 19, :] = hrecv[e, 48 + q * 16 : 64 + q * 16].astype(f32) * m_rt

        def step(i, _):
            extend_row(x, 3 + 2 * i)
            extend_row(x, 4 + 2 * i)
            return 0

        lax.fori_loop(0, TR // 2, step, 0)

    def fill_rows(e, x):
        await_bytes(hrecv.at[e, pl.ds(96, 448)], hr_sem.at[e])
        corners = hrecv[e, 480:544].astype(f32)
        for q in range(3):
            x[q * ROWV + 24 : q * ROWV + 88, :] = hrecv[e, 96 + q * 64 : 160 + q * 64].astype(f32) * m_up
            x[(19 + q) * ROWV + 24 : (19 + q) * ROWV + 88, :] = (
                hrecv[e, 288 + q * 64 : 352 + q * 64].astype(f32) * m_dn
            )
            o = q * 24
            for c, (ref, m, at) in enumerate(
                ((lf, m_lt * m_up, o), (rf, m_rt * m_up, o), (lf, m_lt * m_dn, o + 19), (rf, m_rt * m_dn, o + 19))
            ):
                ref[at : at + 3, :] = corners[c * 16 + q * 4 : c * 16 + q * 4 + 3] * m

        def step(i, _):
            extend_row(x, i)
            extend_row(x, i + 19)
            return 0

        lax.fori_loop(0, 3, step, 0)

    def conv_rows(x, layer, r, count, flip):
        accs = [None] * count
        for a in range(6 + count):
            xa = x[rows((r + a) * ROWV, ROWV), :].reshape(14, 8, LN)
            for b in range(7):
                for n in range(count):
                    if 0 <= a - n < 7:
                        tap = (6 - a + n) * 8 + 6 - b if flip else (a - n) * 8 + b
                        term = xa[b : b + 8] * kb[layer, tap][None]
                        accs[n] = term if accs[n] is None else accs[n] + term
        return accs

    stage[...] = jnp.zeros_like(stage)
    corner[...] = jnp.zeros_like(corner)
    loads[0].wait()
    stage[:, 0:CH] = img_in[...].astype(f32)

    def spread(r, _):
        for j in range(8):
            x0[rows((r + 3) * ROWV + (3 + j) * 8, 8), :] = stage[pl.ds(r * TC + j, 8, stride=8), :]
        return 0

    lax.fori_loop(0, TR, spread, 0)
    pack_halo(0, x0)
    pl.semaphore_wait(barrier, len(everyone))
    start_halo(0)

    gb[...] = jnp.zeros_like(gb)
    ub[...] = jnp.zeros_like(ub)
    db[...] = jnp.zeros_like(db)
    kb[...] = jnp.zeros_like(kb)
    gain[...] = jnp.zeros_like(gain)
    sacc[...] = jnp.zeros_like(sacc)
    wsum[...] = jnp.zeros_like(wsum)
    wa[...] = jnp.zeros_like(wa)
    for load in loads[1:]:
        load.wait()
    for layer in range(2):
        gb[layer, 0:1, 0:CH] = g_in[layer : layer + 1, :]
        ub[layer, 0:CH, :] = u_in[layer]
        db[layer, 0:CH, :] = d_in[layer]
        for a in range(7):
            for b in range(7):
                kb[layer, a * 8 + b, :, 0:CH] = jnp.broadcast_to(k_in[a, b, layer : layer + 1, :], (8, CH))
    o, k = iota((192, 256), 0), iota((192, 256), 1)
    q = (o * 43691) >> 19
    i = o - q * 12
    pick_rows[...] = (k == ((q >> 1) & 1) * 128 + (q & 1) * 48 + (q >> 2) * 12 + i).astype(f32).astype(bf16)
    for y in range(NY):
        k, n = iota((FF, LN), 0), iota((FF, LN), 1)
        pick_cols[y] = ((k == n + y * 96) & (n < 96)).astype(f32).astype(bf16)
    o, k = iota((LN, LN), 0), iota((LN, LN), 1)
    pick_units[...] = ((k == (o >> 4) * 12 + (o & 15)) & ((o & 15) < 12)).astype(f32).astype(bf16)
    stage[:, 0:CH] = cot_in[...].astype(f32)

    def spread_cot(r, _):
        for j in range(8):
            gradf[rows(r * TC + j * 8, 8), :] = stage[pl.ds(r * TC + j, 8, stride=8), :]
        return 0

    lax.fori_loop(0, TR, spread_cot, 0)
    lane_ok = jnp.where(iota((8, LN), 1) < CH, 1.0, 0.0).astype(f32)[0:1]

    INNER = ((3, 10),)
    OUTER = ((0, 3), (13, 3))

    def part(inner, conv_step, mix_step):
        if conv_step is not None:
            if inner:
                lax.fori_loop(0, 5, lambda i, c: (conv_step(3 + 2 * i, 2), c)[1], 0)
            else:
                lax.fori_loop(0, 2, lambda i, c: (conv_step(13 * i, 3), c)[1], 0)
        if mix_step is not None:
            mix_step(INNER if inner else OUTER)

    def take(ref, spans):
        return jnp.concatenate([ref[r * TC : (r + n) * TC, :] for r, n in spans], axis=0)

    def put(ref, spans, value):
        at = 0
        for r, n in spans:
            ref[r * TC : (r + n) * TC, :] = value[at : at + n * TC]
            at += n * TC

    def listed(spans):
        return [r + k for r, n in spans for k in range(n)]

    def forward(layer, inner):
        x = xs[layer]

        def conv_step(r, count):
            for n, acc in enumerate(conv_rows(x, layer, r, count, False)):
                conv[rows((r + n) * TC, TC), :] = acc.reshape(TC, LN)

        def mix(spans):
            v = take(conv, spans)
            mean = jnp.sum(v, axis=1, keepdims=True) * (1.0 / CH)
            centred = (v - mean) * lane_ok
            variance = jnp.sum(centred * centred, axis=1, keepdims=True) * (1.0 / CH)
            inverse = lax.rsqrt(variance + epsilon)
            u = centred * inverse
            put(unit.at[layer], spans, u)
            put(inv.at[layer], spans, jnp.broadcast_to(inverse, u.shape))
            n = (u * gb[layer, 0:1, :]).astype(bf16)
            put(normed.at[layer], spans, n)
            pre = dot(n, ub[layer], 1, 0)
            e = jnp.exp2(pre * pre * half_log2e)
            t = reciprocal(1.0 + tail_p * jnp.abs(pre))
            poly = tail_c[5] * t + tail_c[4]
            for k in (3, 2, 1, 0):
                poly = poly * t + tail_c[k]
            tail = poly * (t * e)
            cdf = jnp.where(pre >= 0.0, 1.0 - tail, tail)
            h = (pre * cdf).astype(bf16)
            put(hidden.at[layer], spans, h)
            put(slope.at[layer], spans, cdf + pre * (e * inv_sqrt_two_pi))
            branch = dot(h, db[layer], 1, 1)
            for n, r in enumerate(listed(spans)):
                start = (r + 3) * ROWV + 24
                value = (x[start : start + TC, :] + branch[n * TC : n * TC + TC]).astype(bf16).astype(f32)
                if layer == 0:
                    x1[start : start + TC, :] = value
                else:
                    for j in range(8):
                        stage[pl.ds(r * TC + j, 8, stride=8), :] = value[j * 8 : j * 8 + 8]

        part(inner, conv_step, mix)

    def backward(layer, inner):
        g = gs[layer]

        def mix(spans):
            gr = take(gradf, spans).astype(bf16)
            put(gradb, spans, gr)
            pg = (dot(gr, db[layer], 1, 0) * take(slope.at[layer], spans)).astype(bf16)
            put(pregrad, spans, pg)
            ng = dot(pg, ub[layer], 1, 1)
            u = take(unit.at[layer], spans)
            gain[layer] += jnp.sum((ng * u).reshape(u.shape[0] // 8, 8, LN), axis=0)
            m = ng * gb[layer, 0:1, :]
            mean_m = jnp.sum(m, axis=1, keepdims=True) * (1.0 / CH)
            mean_mu = jnp.sum(m * u, axis=1, keepdims=True) * (1.0 / CH)
            cg = take(inv.at[layer], spans) * (m - mean_m - u * mean_mu)
            cg = cg.astype(bf16).astype(f32)
            for n, r in enumerate(listed(spans)):
                start = (r + 3) * ROWV + 24
                g[start : start + TC, :] = cg[n * TC : n * TC + TC]

        part(inner, None, mix)

    def input_grad(layer, inner):
        def step(r, count):
            for n, acc in enumerate(conv_rows(gs[layer], layer, r, count, True)):
                here = rows((r + n) * TC, TC)
                value = (gradf[here, :] + acc.reshape(TC, LN)).astype(bf16).astype(f32)
                if layer == 1:
                    gradf[here, :] = value
                else:
                    for j in range(8):
                        stage[pl.ds((r + n) * TC + j, 8, stride=8), :] = value[j * 8 : j * 8 + 8]

        part(inner, step, None)

    def weight_sums(layer):
        up_sum = dot(normed[layer], pregrad[...], 0, 0)
        down_sum = dot(gradb[...], hidden[layer], 0, 0)
        both = jnp.concatenate([up_sum, down_sum], axis=0).astype(bf16)
        ordered = dot(pick_rows[...], both, 1, 0).astype(bf16)
        for y in range(NY):
            sblk[layer, y] = dot(ordered, pick_cols[y], 1, 0).astype(bf16)

    def send_blocks(layer):
        for d in range(1, GROUP):
            ox, oy, device = peer_a(d)
            send(
                sblk.at[layer, oy, pl.ds(pl.multiple_of(ox * 48, 16), 48)],
                rblk.at[layer, d - 1],
                s1_sem.at[layer],
                r1_sem.at[layer],
                device,
            )

    def gather_blocks(layer):
        await_bytes(rblk.at[layer], r1_sem.at[layer])
        total = sblk[layer, py, pl.ds(pl.multiple_of(px * 48, 16), 48)].astype(f32)
        for d in range(1, GROUP):
            total = total + rblk[layer, d - 1].astype(f32)
        sacc[layer * 48 : layer * 48 + 48, :] = total

    def kernel_sums(layer, inner):
        x, g = xs[layer], gs[layer]

        def products(r, a):
            xa = x[rows((r + a) * ROWV, ROWV), :].reshape(14, 8, LN)
            gr = g[rows((r + 3) * ROWV + 24, TC), :].reshape(8, 8, LN)
            return tuple(jnp.sum(xa[b : b + 8] * gr, axis=0) for b in range(7))

        def tap_row(a, _):
            here = pl.ds(pl.multiple_of(a * 64, 64), 56)
            if inner:
                zero = tuple(jnp.zeros((8, LN), f32) for _ in range(7))
                acc = lax.fori_loop(
                    0, 2, lambda i, acc: fold(acc, [products(3 + 5 * i + n, a) for n in range(5)]), zero
                )
                wsum[here, :] = jnp.concatenate(acc, axis=0)
            else:
                acc = tuple(wsum[pl.ds(pl.multiple_of(a * 64 + b * 8, 8), 8), :] for b in range(7))
                acc = fold(acc, [products(r, a) for r in listed(OUTER)])
                wsum[here, :] = jnp.concatenate(acc, axis=0)
            return 0

        def fold(acc, terms):
            for term in terms:
                acc = tuple(p + q for p, q in zip(acc, term))
            return acc

        lax.fori_loop(0, 7, tap_row, 0)
        if not inner:
            wsum[56:64, :] = gain[layer]
            for a in range(7):
                wa[layer, a * 8 : a * 8 + 8, :] = jnp.sum(wsum[a * 64 : a * 64 + 64, :].reshape(8, 8, LN), axis=1)

    mine_a, mine_z = px * NY + py, zh * (NZC // 2) + zc // 2
    own = pl.ds(pl.multiple_of(core * 32, 32), 32)
    other = pl.ds(pl.multiple_of(32 - core * 32, 32), 32)

    def pair_send(layer):
        send(wa.at[layer, other], wpair.at[layer], ps_sem.at[layer], pr_sem.at[layer], pair)

    def group_send(layer):
        await_bytes(wpair.at[layer], pr_sem.at[layer])
        wgroup[layer, mine_a] = (wa[layer, own, :] + wpair[layer]).astype(bf16)
        for d in range(1, GROUP):
            block = wgroup.at[layer, mine_a]
            send(block, block, as_sem.at[layer], ar_sem.at[layer], peer_a(d)[2])

    def line_send(layer):
        await_bytes(wgroup.at[layer, pl.ds(0, GROUP - 1)], ar_sem.at[layer])
        total = wgroup[layer, 0].astype(f32)
        for d in range(1, GROUP):
            total = total + wgroup[layer, d].astype(f32)
        wline[layer, mine_z] = total.astype(bf16)
        for d in range(1, 8):
            block = wline.at[layer, mine_z]
            send(block, block, zs_sem.at[layer], zr_sem.at[layer], peer_b((d // 4) * 8 + (d % 4) * 2)[1])

    def return_send(layer):
        await_bytes(wline.at[layer, pl.ds(0, 7)], zr_sem.at[layer])
        total = wline[layer, 0].astype(f32)
        for d in range(1, 8):
            total = total + wline[layer, d].astype(f32)
        wall[layer, own, :] = total * (1.0 / 512.0)
        send(wall.at[layer, own], wall.at[layer, own], cs_sem.at[layer], cr_sem.at[layer], pair)

    fill_cols(0, x0)
    forward(0, True)
    fill_rows(0, x0)
    forward(0, False)
    pack_halo(1, x1)
    start_halo(1)

    fill_cols(1, x1)
    forward(1, True)
    backward(1, True)
    fill_rows(1, x1)
    forward(1, False)
    backward(1, False)
    pack_halo(2, g1)
    start_halo(2)

    weight_sums(1)
    send_blocks(1)
    kernel_sums(1, True)
    kernel_sums(1, False)
    pair_send(1)
    out[...] = stage[:, 0:CH].astype(bf16)
    group_send(1)

    fill_cols(2, g1)
    input_grad(1, True)
    backward(0, True)
    kernel_sums(0, True)
    fill_rows(2, g1)
    input_grad(1, False)
    backward(0, False)
    kernel_sums(0, False)
    pair_send(0)
    weight_sums(0)
    group_send(0)
    send_blocks(0)
    pack_halo(3, g0)
    start_halo(3)
    line_send(1)
    gather_blocks(1)

    fill_cols(3, g0)
    input_grad(0, True)

    line_send(0)

    gather_blocks(0)
    s2blk[...] = dot(pick_units[...], sacc[...].astype(bf16), 1, 1).astype(bf16)
    for d in range(1, GROUP):
        oz, device = peer_b(d)
        send(
            s2blk.at[pl.ds(pl.multiple_of(oz * 16, 16), 16)], r2blk.at[pl.ds((d - 1) * 16, 16)], s2_sem, r2_sem, device
        )

    fill_rows(3, g0)
    input_grad(0, False)
    gimg[...] = stage[:, 0:CH].astype(bf16)

    return_send(1)
    return_send(0)

    await_bytes(r2blk, r2_sem)
    total = s2blk[pl.ds(pl.multiple_of(zc * 16, 16), 16), :].astype(f32)
    for d in range(1, GROUP):
        total = total + r2blk[(d - 1) * 16 : d * 16, :].astype(f32)
    total = total * (1.0 / 512.0)
    turned = jnp.concatenate([total, jnp.zeros((LN - 16, LN), f32)], axis=0).T
    for layer in range(2):
        o = layer * 48
        gup[:, layer, :] = jnp.where(zh == 0, turned[o : o + 12, 0:12], turned[o + 12 : o + 24, 0:12])
        gdown[:, layer, :] = jnp.where(zh == 0, total[0:12, o + 24 : o + 36], total[0:12, o + 36 : o + 48])

    for layer in range(2):
        await_bytes(wall.at[layer, pl.ds(0, 32)], cr_sem.at[layer])
        for a in range(7):
            gker[a, :, layer, :] = wall[layer, a * 8 : a * 8 + 7, 0:CH]
        ggain[layer : layer + 1, :] = wall[layer, 7:8, 0:CH]

    for e in range(4):
        await_bytes(hsend.at[e], hs_sem.at[e])
    for layer in range(2):
        await_bytes(rblk.at[layer], s1_sem.at[layer])
    await_bytes(r2blk, s2_sem)
    for layer in range(2):
        await_bytes(wpair.at[layer], ps_sem.at[layer])
        await_bytes(wgroup.at[layer, pl.ds(0, GROUP - 1)], as_sem.at[layer])
        await_bytes(wline.at[layer, pl.ds(0, 7)], zs_sem.at[layer])
        await_bytes(wall.at[layer, pl.ds(0, 32)], cs_sem.at[layer])


def place(*refs):
    for source, target in zip(refs[:6], refs[6:]):
        target[...] = source[...]


def per_device(image, kernels, gains, ups, downs, cot):
    vmem = pltpu.VMEM
    dma = pltpu.SemaphoreType.DMA
    any_spec = pl.BlockSpec(memory_space=pltpu.HBM)
    vmem_spec = pl.BlockSpec(memory_space=pltpu.VMEM)
    outs = pl.pallas_call(
        kernel,
        out_shape=(
            vmem((PX, CH), bf16),
            vmem((PX, CH), bf16),
            vmem((7, 7, 2, CH), f32),
            vmem((2, CH), f32),
            vmem((12, 2, 12), f32),
            vmem((12, 2, 12), f32),
        ),
        in_specs=[any_spec] * 6,
        out_specs=(vmem_spec, vmem_spec, vmem_spec, vmem_spec, vmem_spec, vmem_spec),
        scratch_shapes=[
            vmem((PX, CH), bf16),
            vmem((PX, CH), bf16),
            vmem((PX, CH), bf16),
            vmem((PX, CH), bf16),
            vmem((7, 7, 2, CH), f32),
            vmem((2, CH), f32),
            vmem((2, CH, FF), bf16),
            vmem((2, CH, FF), bf16),
            vmem((PADDED, LN), f32),
            vmem((PADDED, LN), f32),
            vmem((PADDED, LN), f32),
            vmem((PADDED, LN), f32),
            vmem((2, 56, 8, LN), f32),
            vmem((2, 8, LN), f32),
            vmem((2, LN, FF), bf16),
            vmem((2, LN, FF), bf16),
            vmem((PX, LN), f32),
            vmem((PX, LN), f32),
            vmem((PX, LN), f32),
            vmem((2, PX, LN), f32),
            vmem((2, PX, LN), f32),
            vmem((2, PX, LN), bf16),
            vmem((2, PX, FF), bf16),
            vmem((2, PX, FF), f32),
            vmem((PX, FF), bf16),
            vmem((PX, LN), bf16),
            vmem((72, LN), f32),
            vmem((72, LN), f32),
            vmem((64, LN), f32),
            vmem((4, HALO, LN), bf16),
            vmem((4, HALO, LN), bf16),
            vmem((2, 8, LN), f32),
            vmem((192, 256), bf16),
            vmem((NY, FF, LN), bf16),
            vmem((LN, LN), bf16),
            vmem((7 * 64, LN), f32),
            vmem((2, NY, 192, LN), bf16),
            vmem((2, GROUP - 1, 48, LN), bf16),
            vmem((LN, LN), f32),
            vmem((LN, LN), bf16),
            vmem(((GROUP - 1) * 16, LN), bf16),
            vmem((2, 64, LN), f32),
            vmem((2, 32, LN), f32),
            vmem((2, GROUP, 32, LN), bf16),
            vmem((2, 8, 32, LN), bf16),
            vmem((2, 64, LN), f32),
            dma((6,)),
            dma((2,)),
            dma((4,)),
            dma((4,)),
            dma((4,)),
            dma((2,)),
            dma((2,)),
            dma,
            dma,
        ]
        + [dma((2,))] * 8,
        compiler_params=pltpu.CompilerParams(
            collective_id=0, has_side_effects=True, vmem_limit_bytes=56 * 1024 * 1024
        ),
        cost_estimate=pl.CostEstimate(flops=2000000000, bytes_accessed=2000000, transcendentals=1600000),
    )(
        *(
            pltpu.with_memory_space_constraint(array, pltpu.HBM)
            for array in (
                image.reshape(PX, CH),
                kernels.transpose(1, 2, 0, 3),
                gains,
                ups,
                downs.transpose(0, 2, 1),
                cot.reshape(PX, CH),
            )
        )
    )
    outs = pl.pallas_call(
        place,
        out_shape=tuple(jax.ShapeDtypeStruct(o.shape, o.dtype) for o in outs),
        in_specs=[vmem_spec] * 6,
        out_specs=(vmem_spec,) * 6,
    )(*(pltpu.with_memory_space_constraint(o, pltpu.VMEM) for o in outs))
    return (
        outs[0].reshape(TR, TC, CH),
        outs[1].reshape(TR, TC, CH),
        outs[2].transpose(2, 0, 1, 3),
        outs[3],
        outs[4].transpose(1, 0, 2),
        outs[5].transpose(1, 0, 2),
    )


def solution(mesh):
    placed = (P("row", "col", None), P(), P(), P(), P(), P("row", "col", None))
    return jax.shard_map(
        per_device,
        mesh=mesh,
        in_specs=placed,
        out_specs=(
            P("row", "col", None),
            P("row", "col", None),
            P(),
            P(),
            P(None, "row", "col"),
            P(None, "col", "row"),
        ),
        check_vma=False,
    )
```

```python
import functools
import math

import jax
import jax.numpy as jnp
from jax import lax
from jax.experimental import pallas as pl
from jax.experimental.pallas import tpu as pltpu
from jax.sharding import PartitionSpec as P

f32 = jnp.float32
bf16 = jnp.bfloat16
MESH = pl.DeviceIdType.MESH

epsilon = 1e-06
inv_sqrt_two_pi = 0.3989422804014327
half_log2e = -0.7213475204444817
tail_p = 0.275
tail_c = (
    0.11780924948816489,
    0.04211150374007564,
    0.33393224058082305,
    -0.33099335173379324,
    0.45199869046687746,
    -0.11485832782346941,
)

NX, NZH, NY, NZC = 4, 2, 4, 8
TR, TC, CH, FF, LN = 16, 64, 96, 384, 128
PX = TR * TC
ROWV = 14 * 8
PADDED = 22 * ROWV
HALO = 544
GROUP = 16


def reciprocal(d):
    return pltpu.reciprocal(d, approx=True)


def dot(a, b, ca, cb):
    return lax.dot_general(a, b, (((ca,), (cb,)), ((), ())), preferred_element_type=f32)


def iota(shape, dim):
    return lax.broadcasted_iota(jnp.int32, shape, dim)


def kernel(
    image, kernels, gains, ups, downs, cot,
    out, gimg, gker, ggain, gup, gdown,
    img_in, cot_in, out_b, gimg_b, k_in, g_in, u_in, d_in,
    x0, x1, g0, g1, kb, gb, ub, db, stage, gradf, conv, unit, inv, normed, hidden, slope, pregrad, gradb,
    lf, rf, corner, hsend, hrecv, gain, pick_rows, pick_cols, pick_units, wsum, sblk, rblk, sacc, s2blk, r2blk, wa, wpair, wgroup, wline, wall,
    in_sem, out_sem, hs_sem, hc_sem, hr_sem, s1_sem, r1_sem, s2_sem, r2_sem, ps_sem, pr_sem, as_sem, ar_sem,
    zs_sem, zr_sem, cs_sem, cr_sem,
):
    xs = (x0, x1)
    gs = (g0, g1)
    ri = lax.axis_index("row")
    ci = lax.axis_index("col")
    zh, px = ri // NX, ri % NX
    py, zc = ci // NZC, ci % NZC
    core = ci % 2
    nrow, ncol = NX * NZH, NY * NZC

    def peer_a(d):
        ox = (px + d // NY) % NX
        oy = (py + d % NY) % NY
        return ox, oy, (zh * NX + ox, oy * NZC + zc)

    def peer_b(d):
        oh = (zh + d // NZC) % NZH
        oz = (zc + d % NZC) % NZC
        return oz, (oh * NX + px, py * NZC + oz)

    def send(src, dst, send_sem, recv_sem, device):
        pltpu.make_async_remote_copy(
            src_ref=src, dst_ref=dst, send_sem=send_sem, recv_sem=recv_sem, device_id=device, device_id_type=MESH
        ).start()

    def await_bytes(ref, sem):
        pltpu.make_async_copy(ref, ref, sem).wait()

    up_r, dn_r = (ri + nrow - 1) % nrow, (ri + 1) % nrow
    lt_c, rt_c = (ci + ncol - 1) % ncol, (ci + 1) % ncol
    pair = (ri, ci + 1 - 2 * core)

    loads = [
        pltpu.make_async_copy(src, dst, in_sem.at[i])
        for i, (src, dst) in enumerate(
            ((image, img_in), (kernels, k_in), (gains, g_in), (ups, u_in), (downs, d_in), (cot, cot_in))
        )
    ]
    for load in loads:
        load.start()

    barrier = pltpu.get_barrier_semaphore()
    near = [(up_r, ci), (dn_r, ci), (ri, lt_c), (ri, rt_c), (up_r, lt_c), (up_r, rt_c), (dn_r, lt_c), (dn_r, rt_c)]
    everyone = near + [peer_a(d)[2] for d in range(1, GROUP)] + [peer_b(d)[1] for d in range(1, GROUP)]
    for device in everyone:
        pl.semaphore_signal(barrier, inc=1, device_id=device, device_id_type=MESH)

    def rows(start, size):
        return pl.ds(pl.multiple_of(start, 8), size)

    def pack_halo(e, x):
        for q in range(3):
            left, right = (3 + q) * 8, (8 + q) * 8 + 7
            hsend[e, q * 16 : q * 16 + 16] = x[pl.ds(3 * ROWV + left, TR, stride=ROWV), :].astype(bf16)
            hsend[e, 48 + q * 16 : 64 + q * 16] = x[pl.ds(3 * ROWV + right, TR, stride=ROWV), :].astype(bf16)
            top, bottom = (3 + q) * ROWV + 24, (16 + q) * ROWV + 24
            hsend[e, 96 + q * 64 : 160 + q * 64] = x[top : top + 64, :].astype(bf16)
            hsend[e, 288 + q * 64 : 352 + q * 64] = x[bottom : bottom + 64, :].astype(bf16)
            for c, start in enumerate(
                (3 * ROWV + left, 3 * ROWV + right, 16 * ROWV + left, 16 * ROWV + right)
            ):
                corner[c * 16 + q * 4 : c * 16 + q * 4 + 3, :] = x[pl.ds(start, 3, stride=ROWV), :]
        hsend[e, 480:544] = corner[...].astype(bf16)

    def start_halo(e):
        for source, size, target, sem, device in (
            (0, 48, 48, hc_sem, (ri, lt_c)),
            (48, 48, 0, hc_sem, (ri, rt_c)),
            (480, 16, 528, hr_sem, (up_r, lt_c)),
            (496, 16, 512, hr_sem, (up_r, rt_c)),
            (512, 16, 496, hr_sem, (dn_r, lt_c)),
            (528, 16, 480, hr_sem, (dn_r, rt_c)),
            (96, 192, 288, hr_sem, (up_r, ci)),
            (288, 192, 96, hr_sem, (dn_r, ci)),
        ):
            send(hsend.at[e, pl.ds(source, size)], hrecv.at[e, pl.ds(target, size)], hs_sem.at[e], sem.at[e], device)

    m_up = jnp.where(ri == 0, 0.0, 1.0).astype(f32)
    m_dn = jnp.where(ri == nrow - 1, 0.0, 1.0).astype(f32)
    m_lt = jnp.where(ci == 0, 0.0, 1.0).astype(f32)
    m_rt = jnp.where(ci == ncol - 1, 0.0, 1.0).astype(f32)
    first = iota((8, LN), 0) == 0
    last = iota((8, LN), 0) == 7

    def extend_row(x, r):
        base = r * ROWV
        for q in range(3):
            v = x[rows(base + (8 + q) * 8, 8), :]
            edge = jnp.broadcast_to(lf[pl.ds(q * 24 + r, 1), :], (8, LN))
            x[rows(base + q * 8, 8), :] = jnp.where(first, edge, pltpu.roll(v, 1, 0))
            v = x[rows(base + (3 + q) * 8, 8), :]
            edge = jnp.broadcast_to(rf[pl.ds(q * 24 + r, 1), :], (8, LN))
            x[rows(base + (11 + q) * 8, 8), :] = jnp.where(last, edge, pltpu.roll(v, 7, 0))

    def fill_cols(e, x):
        await_bytes(hrecv.at[e, pl.ds(0, 96)], hc_sem.at[e])
        for q in range(3):
            lf[q * 24 + 3 : q * 24 + 19, :] = hrecv[e, q * 16 : q * 16 + 16].astype(f32) * m_lt
            rf[q * 24 + 3 : q * 24 + 19, :] = hrecv[e, 48 + q * 16 : 64 + q * 16].astype(f32) * m_rt

        def step(i, _):
            extend_row(x, 3 + 2 * i)
            extend_row(x, 4 + 2 * i)
            return 0

        lax.fori_loop(0, TR // 2, step, 0)

    def fill_rows(e, x):
        await_bytes(hrecv.at[e, pl.ds(96, 448)], hr_sem.at[e])
        corners = hrecv[e, 480:544].astype(f32)
        for q in range(3):
            x[q * ROWV + 24 : q * ROWV + 88, :] = hrecv[e, 96 + q * 64 : 160 + q * 64].astype(f32) * m_up
            x[(19 + q) * ROWV + 24 : (19 + q) * ROWV + 88, :] = (
                hrecv[e, 288 + q * 64 : 352 + q * 64].astype(f32) * m_dn
            )
            o = q * 24
            for c, (ref, m, at) in enumerate(
                ((lf, m_lt * m_up, o), (rf, m_rt * m_up, o), (lf, m_lt * m_dn, o + 19), (rf, m_rt * m_dn, o + 19))
            ):
                ref[at : at + 3, :] = corners[c * 16 + q * 4 : c * 16 + q * 4 + 3] * m

        def step(i, _):
            extend_row(x, i)
            extend_row(x, i + 19)
            return 0

        lax.fori_loop(0, 3, step, 0)

    def conv_rows(x, layer, r, count, flip):
        accs = [None] * count
        for a in range(6 + count):
            xa = x[rows((r + a) * ROWV, ROWV), :].reshape(14, 8, LN)
            for b in range(7):
                for n in range(count):
                    if 0 <= a - n < 7:
                        tap = (6 - a + n) * 8 + 6 - b if flip else (a - n) * 8 + b
                        term = xa[b : b + 8] * kb[layer, tap][None]
                        accs[n] = term if accs[n] is None else accs[n] + term
        return accs

    stage[...] = jnp.zeros_like(stage)
    corner[...] = jnp.zeros_like(corner)
    loads[0].wait()
    stage[:, 0:CH] = img_in[...].astype(f32)

    def spread(r, _):
        for j in range(8):
            x0[rows((r + 3) * ROWV + (3 + j) * 8, 8), :] = stage[pl.ds(r * TC + j, 8, stride=8), :]
        return 0

    lax.fori_loop(0, TR, spread, 0)
    pack_halo(0, x0)
    pl.semaphore_wait(barrier, len(everyone))
    start_halo(0)

    gb[...] = jnp.zeros_like(gb)
    ub[...] = jnp.zeros_like(ub)
    db[...] = jnp.zeros_like(db)
    kb[...] = jnp.zeros_like(kb)
    gain[...] = jnp.zeros_like(gain)
    sacc[...] = jnp.zeros_like(sacc)
    wsum[...] = jnp.zeros_like(wsum)
    wa[...] = jnp.zeros_like(wa)
    for load in loads[1:]:
        load.wait()
    for layer in range(2):
        gb[layer, 0:1, 0:CH] = g_in[layer : layer + 1, :]
        ub[layer, 0:CH, :] = u_in[layer]
        db[layer, 0:CH, :] = d_in[layer]
        for a in range(7):
            for b in range(7):
                kb[layer, a * 8 + b, :, 0:CH] = jnp.broadcast_to(k_in[a, b, layer : layer + 1, :], (8, CH))
    o, k = iota((192, 256), 0), iota((192, 256), 1)
    q = (o * 43691) >> 19
    i = o - q * 12
    pick_rows[...] = (k == ((q >> 1) & 1) * 128 + (q & 1) * 48 + (q >> 2) * 12 + i).astype(f32).astype(bf16)
    for y in range(NY):
        k, n = iota((FF, LN), 0), iota((FF, LN), 1)
        pick_cols[y] = ((k == n + y * 96) & (n < 96)).astype(f32).astype(bf16)
    o, k = iota((LN, LN), 0), iota((LN, LN), 1)
    pick_units[...] = ((k == (o >> 4) * 12 + (o & 15)) & ((o & 15) < 12)).astype(f32).astype(bf16)
    stage[:, 0:CH] = cot_in[...].astype(f32)

    def spread_cot(r, _):
        for j in range(8):
            gradf[rows(r * TC + j * 8, 8), :] = stage[pl.ds(r * TC + j, 8, stride=8), :]
        return 0

    lax.fori_loop(0, TR, spread_cot, 0)
    lane_ok = jnp.where(iota((8, LN), 1) < CH, 1.0, 0.0).astype(f32)[0:1]

    INNER = ((3, 10),)
    OUTER = ((0, 3), (13, 3))

    def part(inner, conv_step, mix_step):
        if conv_step is not None:
            if inner:
                lax.fori_loop(0, 5, lambda i, c: (conv_step(3 + 2 * i, 2), c)[1], 0)
            else:
                lax.fori_loop(0, 2, lambda i, c: (conv_step(13 * i, 3), c)[1], 0)
        if mix_step is not None:
            mix_step(INNER if inner else OUTER)

    def take(ref, spans):
        return jnp.concatenate([ref[r * TC : (r + n) * TC, :] for r, n in spans], axis=0)

    def put(ref, spans, value):
        at = 0
        for r, n in spans:
            ref[r * TC : (r + n) * TC, :] = value[at : at + n * TC]
            at += n * TC

    def listed(spans):
        return [r + k for r, n in spans for k in range(n)]

    def conv_inside(layer):
        x = xs[layer]
        lf[...] = jnp.zeros_like(lf)
        rf[...] = jnp.zeros_like(rf)

        def extend(i, _):
            extend_row(x, 3 + 2 * i)
            extend_row(x, 4 + 2 * i)
            return 0

        def step(i, _):
            for n, acc in enumerate(conv_rows(x, layer, 3 + 2 * i, 2, False)):
                conv[rows((3 + 2 * i + n) * TC, TC), :] = acc.reshape(TC, LN)
            return 0

        lax.fori_loop(0, TR // 2, extend, 0)
        lax.fori_loop(0, 5, step, 0)

    def conv_rims(layer):
        def step(i, _):
            r = 3 + i
            sums = [None] * 8
            for a in range(7):
                for q in range(3):
                    edge = jnp.broadcast_to(lf[pl.ds(q * 24 + r + a, 1), :], (8, LN))
                    for j in range(q + 1):
                        term = edge * kb[layer, a * 8 + q - j]
                        sums[j] = term if sums[j] is None else sums[j] + term
                    edge = jnp.broadcast_to(rf[pl.ds(q * 24 + r + a, 1), :], (8, LN))
                    for j in range(5 + q, 8):
                        term = edge * kb[layer, a * 8 + 11 + q - j]
                        sums[j] = term if sums[j] is None else sums[j] + term
            for j in range(8):
                if sums[j] is not None:
                    conv[rows(r * TC + j * 8, 8), :] += jnp.where(first if j < 3 else last, sums[j], 0.0)
            return 0

        lax.fori_loop(0, 10, step, 0)

    def forward(layer, inner):
        x = xs[layer]

        def conv_step(r, count):
            for n, acc in enumerate(conv_rows(x, layer, r, count, False)):
                conv[rows((r + n) * TC, TC), :] = acc.reshape(TC, LN)

        def mix(spans):
            v = take(conv, spans)
            mean = jnp.sum(v, axis=1, keepdims=True) * (1.0 / CH)
            centred = (v - mean) * lane_ok
            variance = jnp.sum(centred * centred, axis=1, keepdims=True) * (1.0 / CH)
            inverse = lax.rsqrt(variance + epsilon)
            u = centred * inverse
            put(unit.at[layer], spans, u)
            put(inv.at[layer], spans, jnp.broadcast_to(inverse, u.shape))
            n = (u * gb[layer, 0:1, :]).astype(bf16)
            put(normed.at[layer], spans, n)
            pre = dot(n, ub[layer], 1, 0)
            e = jnp.exp2(pre * pre * half_log2e)
            t = reciprocal(1.0 + tail_p * jnp.abs(pre))
            poly = tail_c[5] * t + tail_c[4]
            for k in (3, 2, 1, 0):
                poly = poly * t + tail_c[k]
            tail = poly * (t * e)
            cdf = jnp.where(pre >= 0.0, 1.0 - tail, tail)
            h = (pre * cdf).astype(bf16)
            put(hidden.at[layer], spans, h)
            put(slope.at[layer], spans, cdf + pre * (e * inv_sqrt_two_pi))
            branch = dot(h, db[layer], 1, 1)
            for n, r in enumerate(listed(spans)):
                start = (r + 3) * ROWV + 24
                value = (x[start : start + TC, :] + branch[n * TC : n * TC + TC]).astype(bf16).astype(f32)
                if layer == 0:
                    x1[start : start + TC, :] = value
                else:
                    for j in range(8):
                        stage[pl.ds(r * TC + j, 8, stride=8), :] = value[j * 8 : j * 8 + 8]

        if inner:
            conv_rims(layer)
        part(inner, None if inner else conv_step, mix)

    def backward(layer, inner):
        g = gs[layer]

        def mix(spans):
            gr = take(gradf, spans).astype(bf16)
            put(gradb, spans, gr)
            pg = (dot(gr, db[layer], 1, 0) * take(slope.at[layer], spans)).astype(bf16)
            put(pregrad, spans, pg)
            ng = dot(pg, ub[layer], 1, 1)
            u = take(unit.at[layer], spans)
            gain[layer] += jnp.sum((ng * u).reshape(u.shape[0] // 8, 8, LN), axis=0)
            m = ng * gb[layer, 0:1, :]
            mean_m = jnp.sum(m, axis=1, keepdims=True) * (1.0 / CH)
            mean_mu = jnp.sum(m * u, axis=1, keepdims=True) * (1.0 / CH)
            cg = take(inv.at[layer], spans) * (m - mean_m - u * mean_mu)
            cg = cg.astype(bf16).astype(f32)
            for n, r in enumerate(listed(spans)):
                start = (r + 3) * ROWV + 24
                g[start : start + TC, :] = cg[n * TC : n * TC + TC]

        part(inner, None, mix)

    def input_grad(layer, inner):
        def step(r, count):
            for n, acc in enumerate(conv_rows(gs[layer], layer, r, count, True)):
                here = rows((r + n) * TC, TC)
                value = (gradf[here, :] + acc.reshape(TC, LN)).astype(bf16).astype(f32)
                if layer == 1:
                    gradf[here, :] = value
                else:
                    for j in range(8):
                        stage[pl.ds((r + n) * TC + j, 8, stride=8), :] = value[j * 8 : j * 8 + 8]

        part(inner, step, None)

    def weight_sums(layer):
        up_sum = dot(normed[layer], pregrad[...], 0, 0)
        down_sum = dot(gradb[...], hidden[layer], 0, 0)
        both = jnp.concatenate([up_sum, down_sum], axis=0).astype(bf16)
        ordered = dot(pick_rows[...], both, 1, 0).astype(bf16)
        for y in range(NY):
            sblk[layer, y] = dot(ordered, pick_cols[y], 1, 0).astype(bf16)

    def send_blocks(layer):
        for d in range(1, GROUP):
            ox, oy, device = peer_a(d)
            send(
                sblk.at[layer, oy, pl.ds(pl.multiple_of(ox * 48, 16), 48)],
                rblk.at[layer, d - 1],
                s1_sem.at[layer],
                r1_sem.at[layer],
                device,
            )

    def gather_blocks(layer):
        await_bytes(rblk.at[layer], r1_sem.at[layer])
        total = sblk[layer, py, pl.ds(pl.multiple_of(px * 48, 16), 48)].astype(f32)
        for d in range(1, GROUP):
            total = total + rblk[layer, d - 1].astype(f32)
        sacc[layer * 48 : layer * 48 + 48, :] = total

    def kernel_sums(layer, inner):
        x, g = xs[layer], gs[layer]

        def products(r, a):
            xa = x[rows((r + a) * ROWV, ROWV), :].reshape(14, 8, LN)
            gr = g[rows((r + 3) * ROWV + 24, TC), :].reshape(8, 8, LN)
            return tuple(jnp.sum(xa[b : b + 8] * gr, axis=0) for b in range(7))

        def tap_row(a, _):
            here = pl.ds(pl.multiple_of(a * 64, 64), 56)
            if inner:
                zero = tuple(jnp.zeros((8, LN), f32) for _ in range(7))
                acc = lax.fori_loop(
                    0, 2, lambda i, acc: fold(acc, [products(3 + 5 * i + n, a) for n in range(5)]), zero
                )
                wsum[here, :] = jnp.concatenate(acc, axis=0)
            else:
                acc = tuple(wsum[pl.ds(pl.multiple_of(a * 64 + b * 8, 8), 8), :] for b in range(7))
                acc = fold(acc, [products(r, a) for r in listed(OUTER)])
                wsum[here, :] = jnp.concatenate(acc, axis=0)
            return 0

        def fold(acc, terms):
            for term in terms:
                acc = tuple(p + q for p, q in zip(acc, term))
            return acc

        lax.fori_loop(0, 7, tap_row, 0)
        if not inner:
            wsum[56:64, :] = gain[layer]
            for a in range(7):
                wa[layer, a * 8 : a * 8 + 8, :] = jnp.sum(wsum[a * 64 : a * 64 + 64, :].reshape(8, 8, LN), axis=1)

    mine_a, mine_z = px * NY + py, zh * (NZC // 2) + zc // 2
    own = pl.ds(pl.multiple_of(core * 32, 32), 32)
    other = pl.ds(pl.multiple_of(32 - core * 32, 32), 32)

    def pair_send(layer):
        send(wa.at[layer, other], wpair.at[layer], ps_sem.at[layer], pr_sem.at[layer], pair)

    def group_send(layer):
        await_bytes(wpair.at[layer], pr_sem.at[layer])
        wgroup[layer, mine_a] = (wa[layer, own, :] + wpair[layer]).astype(bf16)
        for d in range(1, GROUP):
            block = wgroup.at[layer, mine_a]
            send(block, block, as_sem.at[layer], ar_sem.at[layer], peer_a(d)[2])

    def line_send(layer):
        await_bytes(wgroup.at[layer, pl.ds(0, GROUP - 1)], ar_sem.at[layer])
        total = wgroup[layer, 0].astype(f32)
        for d in range(1, GROUP):
            total = total + wgroup[layer, d].astype(f32)
        wline[layer, mine_z] = total.astype(bf16)
        for d in range(1, 8):
            block = wline.at[layer, mine_z]
            send(block, block, zs_sem.at[layer], zr_sem.at[layer], peer_b((d // 4) * 8 + (d % 4) * 2)[1])

    def return_send(layer):
        await_bytes(wline.at[layer, pl.ds(0, 7)], zr_sem.at[layer])
        total = wline[layer, 0].astype(f32)
        for d in range(1, 8):
            total = total + wline[layer, d].astype(f32)
        wall[layer, own, :] = total * (1.0 / 512.0)
        send(wall.at[layer, own], wall.at[layer, own], cs_sem.at[layer], cr_sem.at[layer], pair)

    conv_inside(0)
    fill_cols(0, x0)
    forward(0, True)
    fill_rows(0, x0)
    forward(0, False)
    pack_halo(1, x1)
    start_halo(1)

    conv_inside(1)
    fill_cols(1, x1)
    forward(1, True)
    backward(1, True)
    fill_rows(1, x1)
    forward(1, False)
    backward(1, False)
    pack_halo(2, g1)
    start_halo(2)

    weight_sums(1)
    send_blocks(1)
    kernel_sums(1, True)
    kernel_sums(1, False)
    pair_send(1)
    out[...] = stage[:, 0:CH].astype(bf16)
    group_send(1)

    fill_cols(2, g1)
    input_grad(1, True)
    backward(0, True)
    kernel_sums(0, True)
    fill_rows(2, g1)
    input_grad(1, False)
    backward(0, False)
    kernel_sums(0, False)
    pair_send(0)
    weight_sums(0)
    group_send(0)
    send_blocks(0)
    pack_halo(3, g0)
    start_halo(3)
    line_send(1)
    gather_blocks(1)

    fill_cols(3, g0)
    input_grad(0, True)

    line_send(0)

    gather_blocks(0)
    s2blk[...] = dot(pick_units[...], sacc[...].astype(bf16), 1, 1).astype(bf16)
    for d in range(1, GROUP):
        oz, device = peer_b(d)
        send(
            s2blk.at[pl.ds(pl.multiple_of(oz * 16, 16), 16)], r2blk.at[pl.ds((d - 1) * 16, 16)], s2_sem, r2_sem, device
        )

    fill_rows(3, g0)
    input_grad(0, False)
    gimg[...] = stage[:, 0:CH].astype(bf16)

    return_send(1)
    return_send(0)

    await_bytes(r2blk, r2_sem)
    total = s2blk[pl.ds(pl.multiple_of(zc * 16, 16), 16), :].astype(f32)
    for d in range(1, GROUP):
        total = total + r2blk[(d - 1) * 16 : d * 16, :].astype(f32)
    total = total * (1.0 / 512.0)
    turned = jnp.concatenate([total, jnp.zeros((LN - 16, LN), f32)], axis=0).T
    for layer in range(2):
        o = layer * 48
        gup[:, layer, :] = jnp.where(zh == 0, turned[o : o + 12, 0:12], turned[o + 12 : o + 24, 0:12])
        gdown[:, layer, :] = jnp.where(zh == 0, total[0:12, o + 24 : o + 36], total[0:12, o + 36 : o + 48])

    for layer in range(2):
        await_bytes(wall.at[layer, pl.ds(0, 32)], cr_sem.at[layer])
        for a in range(7):
            gker[a, :, layer, :] = wall[layer, a * 8 : a * 8 + 7, 0:CH]
        ggain[layer : layer + 1, :] = wall[layer, 7:8, 0:CH]

    for e in range(4):
        await_bytes(hsend.at[e], hs_sem.at[e])
    for layer in range(2):
        await_bytes(rblk.at[layer], s1_sem.at[layer])
    await_bytes(r2blk, s2_sem)
    for layer in range(2):
        await_bytes(wpair.at[layer], ps_sem.at[layer])
        await_bytes(wgroup.at[layer, pl.ds(0, GROUP - 1)], as_sem.at[layer])
        await_bytes(wline.at[layer, pl.ds(0, 7)], zs_sem.at[layer])
        await_bytes(wall.at[layer, pl.ds(0, 32)], cs_sem.at[layer])


def place(*refs):
    for source, target in zip(refs[:6], refs[6:]):
        target[...] = source[...]


def per_device(image, kernels, gains, ups, downs, cot):
    vmem = pltpu.VMEM
    dma = pltpu.SemaphoreType.DMA
    any_spec = pl.BlockSpec(memory_space=pltpu.HBM)
    vmem_spec = pl.BlockSpec(memory_space=pltpu.VMEM)
    outs = pl.pallas_call(
        kernel,
        out_shape=(
            vmem((PX, CH), bf16),
            vmem((PX, CH), bf16),
            vmem((7, 7, 2, CH), f32),
            vmem((2, CH), f32),
            vmem((12, 2, 12), f32),
            vmem((12, 2, 12), f32),
        ),
        in_specs=[any_spec] * 6,
        out_specs=(vmem_spec, vmem_spec, vmem_spec, vmem_spec, vmem_spec, vmem_spec),
        scratch_shapes=[
            vmem((PX, CH), bf16),
            vmem((PX, CH), bf16),
            vmem((PX, CH), bf16),
            vmem((PX, CH), bf16),
            vmem((7, 7, 2, CH), f32),
            vmem((2, CH), f32),
            vmem((2, CH, FF), bf16),
            vmem((2, CH, FF), bf16),
            vmem((PADDED, LN), f32),
            vmem((PADDED, LN), f32),
            vmem((PADDED, LN), f32),
            vmem((PADDED, LN), f32),
            vmem((2, 56, 8, LN), f32),
            vmem((2, 8, LN), f32),
            vmem((2, LN, FF), bf16),
            vmem((2, LN, FF), bf16),
            vmem((PX, LN), f32),
            vmem((PX, LN), f32),
            vmem((PX, LN), f32),
            vmem((2, PX, LN), f32),
            vmem((2, PX, LN), f32),
            vmem((2, PX, LN), bf16),
            vmem((2, PX, FF), bf16),
            vmem((2, PX, FF), f32),
            vmem((PX, FF), bf16),
            vmem((PX, LN), bf16),
            vmem((72, LN), f32),
            vmem((72, LN), f32),
            vmem((64, LN), f32),
            vmem((4, HALO, LN), bf16),
            vmem((4, HALO, LN), bf16),
            vmem((2, 8, LN), f32),
            vmem((192, 256), bf16),
            vmem((NY, FF, LN), bf16),
            vmem((LN, LN), bf16),
            vmem((7 * 64, LN), f32),
            vmem((2, NY, 192, LN), bf16),
            vmem((2, GROUP - 1, 48, LN), bf16),
            vmem((LN, LN), f32),
            vmem((LN, LN), bf16),
            vmem(((GROUP - 1) * 16, LN), bf16),
            vmem((2, 64, LN), f32),
            vmem((2, 32, LN), f32),
            vmem((2, GROUP, 32, LN), bf16),
            vmem((2, 8, 32, LN), bf16),
            vmem((2, 64, LN), f32),
            dma((6,)),
            dma((2,)),
            dma((4,)),
            dma((4,)),
            dma((4,)),
            dma((2,)),
            dma((2,)),
            dma,
            dma,
        ]
        + [dma((2,))] * 8,
        compiler_params=pltpu.CompilerParams(
            collective_id=0, has_side_effects=True, vmem_limit_bytes=56 * 1024 * 1024
        ),
        cost_estimate=pl.CostEstimate(flops=2000000000, bytes_accessed=2000000, transcendentals=1600000),
    )(
        *(
            pltpu.with_memory_space_constraint(array, pltpu.HBM)
            for array in (
                image.reshape(PX, CH),
                kernels.transpose(1, 2, 0, 3),
                gains,
                ups,
                downs.transpose(0, 2, 1),
                cot.reshape(PX, CH),
            )
        )
    )
    outs = pl.pallas_call(
        place,
        out_shape=tuple(jax.ShapeDtypeStruct(o.shape, o.dtype) for o in outs),
        in_specs=[vmem_spec] * 6,
        out_specs=(vmem_spec,) * 6,
    )(*(pltpu.with_memory_space_constraint(o, pltpu.VMEM) for o in outs))
    return (
        outs[0].reshape(TR, TC, CH),
        outs[1].reshape(TR, TC, CH),
        outs[2].transpose(2, 0, 1, 3),
        outs[3],
        outs[4].transpose(1, 0, 2),
        outs[5].transpose(1, 0, 2),
    )


def solution(mesh):
    placed = (P("row", "col", None), P(), P(), P(), P(), P("row", "col", None))
    return jax.shard_map(
        per_device,
        mesh=mesh,
        in_specs=placed,
        out_specs=(
            P("row", "col", None),
            P("row", "col", None),
            P(),
            P(),
            P(None, "row", "col"),
            P(None, "col", "row"),
        ),
        check_vma=False,
    )
```
